768 devices in a mesh: expert: 16 (over y, core), dp: 48 (over z, x).
Axes of the slice: x: 4, y: 8, z: 12, core: 2. Of those that a mesh axis runs over, the one named last changes fastest.
Arguments:
- routes: int32 [98304, 1], P(('expert', 'dp')), may hold values from 0 to 15; in each aligned block of 128 rows (0 to 127, 128 to 255, ...) at most 9 rows name the same one
- residual_grad: bfloat16 [98304, 2048], P(('expert', 'dp')), may hold values from -6 to 6
- saved_inputs: bfloat16 [16, 6912, 2048], P('expert', 'dp'), may hold values from -6 to 6
- saved_preact: bfloat16 [16, 6912, 288], P('expert', 'dp'), may hold values from -6 to 6
- expert_grad: bfloat16 [16, 6912, 2048], P('expert', 'dp'), may hold values from -6 to 6
- w_in: bfloat16 [16, 288, 2048], P('expert'), may hold values from -0.125 to 0.125
- w_out: bfloat16 [16, 288, 2048], P('expert'), may hold values from -0.375 to 0.375
Outputs:
- token_grad: bfloat16 [98304, 2048], P(('expert', 'dp'))
- grad_in: float32 [16, 288, 2048], P('expert', 'dp')
The draws below stay inside these ranges and needn't reach their ends.
Inputs may be any that keep to these rules, and one draw needn't show every extreme that they name: `routes`: in each aligned block of 128 rows (the tokens of one device) no expert is named by more than 9 rows, and in every draw some block names some expert exactly 9 times.
All inputs are finite; a program needn't handle non-finite values.
Results may differ from the reference program's by a relative error of at most 0.0047.
Values may be sent and summed in bfloat16 or wider, within the bound.
No kernel may reach another device: no remote copies, remote signals or barrier semaphores. Data moves between devices by JAX's collectives and lax.ppermute only.
A program may use at most 32 MiB of HBM per device.

```python
import math
import jax
import jax.numpy as jnp
import numpy as np
from jax import lax

D = 2048
UNITS = 288
TOK_DEV = 128
EXPERTS = 16
CAP = 9
TOKENS = 98304
N_DP = 48


def levels(own_key, shape, cuts, low, high):
    gain, own = 1.0, jax.random.fold_in(own_key, 6)
    for position, blocks in cuts:
        heights = jnp.exp(jax.random.uniform(jax.random.fold_in(own, position), (blocks,), jnp.float32, low / len(cuts), high / len(cuts)))
        gain = gain * jnp.repeat(heights, shape[position] // blocks).reshape([-1 if axis == position else 1 for axis in range(len(shape))])
    return gain


def routed_block(stream_key, own, number, rows, count, top, bound, skew):
    order = jax.random.permutation(stream_key, count)
    heavy_load, ordinary = shares(count, rows * top, bound, skew, True), shares(count, rows * top, bound, skew, False)
    places = jnp.arange(count)

    def named(lengths, offset_by):
        used = int((lengths > 0).sum())
        fixed = max(1, used // 4)
        shifted = fixed + (places - fixed + offset_by * (used - fixed)) % max(1, count - fixed)
        return jnp.zeros((count,), jnp.int32).at[order[jnp.where(places < fixed, places, shifted)]].set(jnp.asarray(lengths, jnp.int32))

    lengths = jnp.where(number % 4 == 0, named(heavy_load, number // 4), named(ordinary, number - number // 4 - 1))
    mixed = jax.random.permutation(jax.random.fold_in(own, 3), count)
    source_of, taker = mixed[0:count // 2 * 2:2], mixed[1:count // 2 * 2:2]
    slack = jnp.minimum(lengths[source_of] - 1, bound - lengths[taker]) // 2
    slack = jnp.where((source_of == order[0]) | (taker == order[0]) | (lengths[taker] == 0), 0, jnp.maximum(slack, 0))
    shifted = jax.random.randint(jax.random.fold_in(own, 4), (count // 2,), 0, 1 << 20) % (slack + 1)
    lengths = lengths.at[source_of].add(-shifted).at[taker].add(shifted)
    items = jnp.searchsorted(jnp.cumsum(lengths), jnp.arange(rows * top), side="right").astype(jnp.int32)
    listing = items.reshape(top, rows).T
    listing = listing[jax.random.permutation(jax.random.fold_in(own, 1), rows)]
    offset_by = jax.random.randint(jax.random.fold_in(own, 2), (rows, 1), 0, top)
    return jnp.take_along_axis(listing, (jnp.arange(top)[None, :] + offset_by) % top, axis=1)


def shares(number_of, total, bound, skew, full):
    portions = [(1 << 20) // math.isqrt(grade ** skew) + 1 for grade in range(1, number_of + 1)]
    largest = bound if full else min(bound, max(-(-total // number_of), total * portions[0] // sum(portions)))
    least = 1 if total - largest >= number_of - 1 else 0
    given, spare = [largest] + [least] * (number_of - 1), total - largest - least * (number_of - 1)
    while spare > 0:
        free = [i for i in range(1, number_of) if given[i] < largest] or [i for i in range(1, number_of) if given[i] < bound]
        mass, left = sum([portions[i] for i in free]), spare
        for i in free:
            extra = min(bound - given[i], max(1, left * portions[i] // mass), spare)
            given[i] = given[i] + extra
            spare = spare - extra
    return np.array(given)


def scatter_about(rng, dims, deviation, reach, shards=(), held_as=jnp.bfloat16):
    values = jax.random.normal(rng, dims, jnp.float32) * deviation
    if len(shards) > 0:
        values = levels(rng, dims, shards, -0.22, 0.18) * values
    return jnp.clip(values, min=-reach, max=reach).astype(held_as)


def setup_inputs(seed: int = 0) -> dict:
    keys = jax.random.split(jax.random.key(seed), 8)
    routes_keys = jax.random.split(jax.random.fold_in(keys[0], 1), TOKENS // TOK_DEV)
    routes_turns = jax.random.permutation(jax.random.fold_in(keys[0], 3), TOKENS // TOK_DEV)
    routes = jax.vmap(lambda own, number: routed_block(jax.random.fold_in(keys[0], 2), own, number, TOK_DEV, EXPERTS, 1, CAP, 2))(routes_keys, routes_turns).reshape((TOKENS, 1))
    residual_grad = scatter_about(keys[1], (TOKENS, D), 1.0, 6.0, ((0, 768),))
    saved_inputs = scatter_about(keys[2], (EXPERTS, N_DP * EXPERTS * CAP, D), 1.0, 6.0, ((0, 16), (1, 48)))
    saved_preact = scatter_about(keys[3], (EXPERTS, N_DP * EXPERTS * CAP, UNITS), 1.0, 6.0, ((0, 16), (1, 48)))
    expert_grad = scatter_about(keys[4], (EXPERTS, N_DP * EXPERTS * CAP, D), 1.0, 6.0, ((0, 16), (1, 48)))
    w_in = scatter_about(keys[5], (EXPERTS, UNITS, D), D ** -0.5, 0.125, ((0, 16),))
    w_out = scatter_about(keys[6], (EXPERTS, UNITS, D), UNITS ** -0.5, 0.375, ((0, 16),))
    return {"routes": routes, "residual_grad": residual_grad, "saved_inputs": saved_inputs, "saved_preact": saved_preact, "expert_grad": expert_grad, "w_in": w_in, "w_out": w_out}


def reference(routes, residual_grad, saved_inputs, saved_preact, expert_grad, w_in, w_out):
    blocks = EXPERTS * N_DP
    ids = routes[:, 0].reshape(blocks, TOK_DEV)
    onehot = (ids[:, :, None] == jnp.arange(EXPERTS, dtype=jnp.int32)[None, None, :]).astype(jnp.int32)
    running = jnp.cumsum(onehot, axis=1, dtype=jnp.int32)
    counts = running[:, -1, :]
    slot_of = jnp.sum((running - onehot) * onehot, axis=2, dtype=jnp.int32)
    per_owner = jnp.transpose(counts.reshape(EXPERTS, N_DP, EXPERTS), (2, 1, 0))
    live = jnp.arange(CAP, dtype=jnp.int32)[None, None, None, :] < per_owner[:, :, :, None]
    live = live.reshape(EXPERTS, N_DP * EXPERTS * CAP)

    def one_expert(pack):
        inputs, preact, raw_grad, mask, weight_in, weight_out = pack
        gated = jnp.where(mask[:, None], raw_grad, jnp.zeros_like(raw_grad))
        product = jnp.dot(gated, weight_out.T, preferred_element_type=jnp.float32)
        hidden_grad = jnp.where(preact > 0, product, jnp.zeros_like(product)).astype(jnp.bfloat16)
        part_in = jnp.dot(hidden_grad.T, inputs, preferred_element_type=jnp.float32) / N_DP
        slot_grad = jnp.dot(hidden_grad, weight_in, preferred_element_type=jnp.float32).astype(jnp.bfloat16)
        return part_in, slot_grad

    grad_in, slot_grad = lax.map(one_expert, (saved_inputs, saved_preact, expert_grad, live, w_in, w_out))
    block_ids = jnp.arange(blocks, dtype=jnp.int32)
    source = block_ids // N_DP
    group = block_ids % N_DP
    row = group[:, None] * (EXPERTS * CAP) + source[:, None] * CAP + slot_of
    flat = slot_grad.reshape(EXPERTS * N_DP * EXPERTS * CAP, D)
    picked = flat[(ids * (N_DP * EXPERTS * CAP) + row).reshape(-1)]
    token_grad = (residual_grad.astype(jnp.float32) + picked.astype(jnp.float32)).astype(jnp.bfloat16)
    return token_grad, grad_in
```

```python
import functools
import jax
import jax.numpy as jnp
from jax import lax
from jax.experimental import pallas as pl
from jax.experimental.pallas import tpu as pltpu
from jax.sharding import Mesh, PartitionSpec as P

BF = jnp.bfloat16
F32 = jnp.float32
CAP = 9
X_DEV = 4
VMEM = 48 * 1024 * 1024


def iota(shape, axis):
    return lax.broadcasted_iota(jnp.int32, shape, axis)


def dot(a, b, ca=1, cb=0):
    return lax.dot_general(a, b, (((ca,), (cb,)), ((), ())), preferred_element_type=F32)


def call(body, outs, *args, flops=0):
    size = sum(a.size * a.dtype.itemsize for a in args) + sum(o.size * o.dtype.itemsize for o in outs)
    return pl.pallas_call(
        body,
        out_shape=outs,
        compiler_params=pltpu.CompilerParams(vmem_limit_bytes=VMEM),
        cost_estimate=pl.CostEstimate(flops=flops, bytes_accessed=size, transcendentals=0),
    )(*args)


def count_body(routes, out):
    rows = out.shape[0]
    hit = (iota((rows, routes.shape[1]), 0) >> 2) == routes[...]
    total = jnp.sum(hit.astype(F32), axis=1, keepdims=True)
    out[...] = jnp.broadcast_to(total, out.shape).astype(jnp.int32)


def hidden_body(grad, w_out, preact, hidden, message):
    product = dot(grad[...], w_out[...], 1, 1)
    h = jnp.where(preact[...].astype(F32) > 0, product, 0.0).astype(BF)
    hidden[...] = h
    units, wide = h.shape[1], message.shape[1]
    col = iota((units, wide), 1)
    place = ((col & 7) < 6) & (iota((units, wide), 0) == 6 * (col >> 3) + (col & 7))
    spread = dot(h, place.astype(BF)).astype(BF)
    rows = h.shape[0]
    for i in range(X_DEV):
        message[i * rows : (i + 1) * rows, :] = spread


def slot_body(hidden, w_in, out):
    rows = hidden.shape[0]
    k = iota((256, rows), 0)
    j = k & 127
    i = iota((256, rows), 1)
    source = 9 * (j >> 3) + jnp.where(k < 128, j & 7, 8)
    picked = dot((i == source).astype(BF), hidden[...]).astype(BF)
    width = w_in.shape[1]
    product = dot(picked, w_in[...])
    out[:, :width] = product[:128].astype(BF)
    row = iota((128, 256), 0) & 7
    last = jnp.zeros((128, 256), F32)
    for r in range(8):
        last = jnp.where(row == r, product[128:, 256 * r : 256 * r + 256], last)
    out[:, width:] = last.astype(BF)


def weight_body(hidden, inputs, counts, out):
    rows = hidden.shape[0]
    n = counts.shape[0]
    eye = (iota((n, n), 0) == iota((n, n), 1)).astype(BF)
    lanes = dot(counts[...].astype(F32).astype(BF), eye, 0, 0)[0:1, :].astype(jnp.int32)
    k = iota((rows, n), 1)
    first = (k & 3) * (rows // X_DEV) + CAP * (k >> 2)
    g = iota((rows, n), 0)
    live = ((g >= first) & (g < first + lanes)).astype(BF)
    mask = dot(live, jnp.ones((n, 128), BF))
    mask = jnp.concatenate([mask] * 3, axis=1)
    h = jnp.where(mask > 0.5, hidden[...].astype(F32), 0.0).astype(BF)
    part = dot(h, inputs[...], 0, 0)
    last = part[:, 384:]
    sub = iota(last.shape, 0) & 7
    for w in range(3):
        tile = part[:, 128 * w : 128 * w + 128]
        tile = jnp.where(sub == 6, pltpu.roll(last, 6 - w, 0), tile)
        tile = jnp.where(sub == 7, pltpu.roll(last, 4 - w, 0), tile)
        out[:, 128 * w : 128 * w + 128] = tile.astype(BF)


def sum_body(scale, parts, out):
    step = 8 * X_DEV
    total = parts[0:step, :].astype(F32)
    for z in range(1, parts.shape[0] // step):
        total = total + parts[z * step : (z + 1) * step, :].astype(F32)
    total = total / scale
    for x in range(X_DEV):
        out[:, 512 * x : 512 * x + 384] = total[8 * x : 8 * x + 6, :]
        for u in range(6):
            v, w = u // 3, u % 3
            out[u : u + 1, 512 * x + 384 : 512 * x + 512] = total[
                8 * x + 6 + v : 8 * x + 7 + v, 128 * w : 128 * w + 128
            ]


def token_body(routes, residual, returned, out):
    ids = routes[...]
    n = ids.shape[1]
    onehot = (iota((16, n), 0) == ids).astype(F32)
    before = (iota((n, n), 0) < iota((n, n), 1)).astype(BF)
    prefix = dot(onehot.astype(BF), before)
    slot = jnp.sum(onehot * prefix, axis=0, keepdims=True).astype(jnp.int32)
    k = iota((n, n), 0)
    same = (k >> 3) == ids
    pick = (same & ((k & 7) == slot)).astype(BF)
    extra = returned[:, 2048:]
    for r in range(8):
        span = slice(256 * r, 256 * r + 256)
        pick_last = (same & (slot == 8) & ((k & 7) == r)).astype(BF)
        got = dot(pick, returned[:, span], 0, 0) + dot(pick_last, extra, 0, 0)
        out[:, span] = (residual[:, span].astype(F32) + got).astype(BF)


def shards(routes, residual_grad, saved_inputs, saved_preact, expert_grad, w_in, w_out):
    S = jax.ShapeDtypeStruct
    inputs = saved_inputs[0]
    slots, width = inputs.shape
    units = w_in.shape[1]
    groups = lax.axis_size("z") * lax.axis_size("x")
    ids = routes.reshape(1, 128)
    (counts,) = call(count_body, [S((64, 128), jnp.int32)], ids)
    counts = lax.all_to_all(
        counts.reshape(64, 1, 128), ("expert", "x"), split_axis=0, concat_axis=0, tiled=True
    ).reshape(64, 128)
    inputs = lax.all_to_all(inputs, "x", split_axis=1, concat_axis=0, tiled=True)
    hidden, message = call(
        hidden_body,
        [S((slots, units), BF), S((X_DEV * slots, 384), BF)],
        expert_grad[0], w_out[0], saved_preact[0],
        flops=2 * slots * units * width,
    )
    message = lax.all_to_all(message, "x", split_axis=0, concat_axis=0, tiled=True)
    (slot_grad,) = call(
        slot_body, [S((128, width + 256), BF)], hidden, w_in[0], flops=4 * 128 * units * width
    )
    returned = lax.all_to_all(slot_grad, "expert", split_axis=0, concat_axis=0, tiled=True)
    (part,) = call(
        weight_body, [S((8 * groups, 384), BF)], message, inputs, counts,
        flops=2 * 576 * 384 * 512,
    )
    part = lax.all_to_all(part, ("z", "x"), split_axis=0, concat_axis=0, tiled=True)
    (token_grad,) = call(
        token_body, [S((128, width), BF)], ids, residual_grad, returned,
        flops=4 * 128 * 128 * width,
    )
    (grad_in,) = call(
        functools.partial(sum_body, float(groups)), [S((6, width), F32)], part
    )
    return token_grad, grad_in[None]


def solution(mesh):
    fine = Mesh(mesh.devices.reshape(16, 12, X_DEV), ("expert", "z", "x"))
    tokens = P(("expert", "z", "x"), None)
    buffers = P("expert", ("z", "x"), None)
    weights = P("expert", None, None)
    return jax.shard_map(
        shards,
        mesh=fine,
        in_specs=(tokens, tokens, buffers, buffers, buffers, weights, weights),
        out_specs=(tokens, buffers),
        check_vma=False,
    )
```

```python
import functools
import jax
import jax.numpy as jnp
from jax import lax
from jax.experimental import pallas as pl
from jax.experimental.pallas import tpu as pltpu
from jax.sharding import Mesh, PartitionSpec as P

BF = jnp.bfloat16
F32 = jnp.float32
CAP = 9
X_DEV = 4
PARTS = 4
MIB = 1024 * 1024


def iota(shape, axis):
    return lax.broadcasted_iota(jnp.int32, shape, axis)


def dot(a, b, ca=1, cb=0):
    return lax.dot_general(a, b, (((ca,), (cb,)), ((), ())), preferred_element_type=F32)


def call(body, outs, *args, flops=0, limit=32, **more):
    size = sum(a.size * a.dtype.itemsize for a in args) + sum(o.size * o.dtype.itemsize for o in outs)
    return pl.pallas_call(
        body,
        out_shape=outs,
        compiler_params=pltpu.CompilerParams(vmem_limit_bytes=limit * MIB),
        cost_estimate=pl.CostEstimate(flops=flops, bytes_accessed=size, transcendentals=0),
        **more,
    )(*args)


def front_body(
    me, grad, w_out, preact, w_in, inputs,
    send0, send1, send2, send3, slots,
    grad_v, w_out_v, preact_v, w_in_v, inputs_v, sems,
):
    width = grad.shape[1]
    part = width // PARTS
    copies = []
    for i in range(PARTS):
        span = pl.ds(i * part, part)
        copies.append(pltpu.make_async_copy(grad.at[:, span], grad_v.at[:, span], sems.at[2 * i]))
        copies.append(pltpu.make_async_copy(w_out.at[:, span], w_out_v.at[:, span], sems.at[2 * i + 1]))
    n = 2 * PARTS
    preact_copy = pltpu.make_async_copy(preact, preact_v, sems.at[n])
    w_in_copy = pltpu.make_async_copy(w_in, w_in_v, sems.at[n + 1])
    inputs_copy = pltpu.make_async_copy(inputs, inputs_v, sems.at[n + 2])
    for c in copies:
        c.start()
    preact_copy.start()
    w_in_copy.start()
    inputs_copy.start()
    rows, units = preact_v.shape
    product = jnp.zeros((rows, units), F32)
    for i in range(PARTS):
        copies[2 * i].wait()
        copies[2 * i + 1].wait()
        span = slice(i * part, i * part + part)
        product = product + dot(grad_v[:, span], w_out_v[:, span], 1, 1)
    preact_copy.wait()
    h = jnp.where(preact_v[...].astype(F32) > 0, product, 0.0).astype(BF)
    col = iota((units, 384), 1)
    place = ((col & 7) < 6) & (iota((units, 384), 0) == 6 * (col >> 3) + (col & 7))
    spread = dot(h, place.astype(BF)).astype(BF)
    k = iota((256, rows), 0)
    j = k & 127
    source = CAP * (j >> 3) + jnp.where(k < 128, j & 7, 8)
    picked = dot((iota((256, rows), 1) == source).astype(BF), h).astype(BF)
    w_in_copy.wait()
    slots[:, :width] = dot(picked[:128], w_in_v[...]).astype(BF)
    row = iota((128, 256), 0) & 7
    last = jnp.zeros((128, 256), F32)
    for r in range(8):
        got = dot(picked[128:], w_in_v[:, 256 * r : 256 * r + 256])
        last = jnp.where(row == r, got, last)
    slots[:, width:] = last.astype(BF)
    inputs_copy.wait()
    for i, send in enumerate((send0, send1, send2, send3)):
        send[:, :384] = spread
        first = pl.multiple_of(((me[0] + i) & 3) * 512, 512)
        send[:, 384:] = inputs_v[:, pl.ds(first, 512)]


def weight_body(me, own, one, two, three, routes, out):
    both = jnp.concatenate([own[...], one[...], two[...], three[...]], axis=0)
    rows, n = both.shape[0], routes.shape[0]
    hits = (routes[...] == me[1]).astype(F32).astype(BF)
    lanes = dot(jnp.ones((8, 128), BF), hits, 1, 1)[0:1, :].astype(jnp.int32)
    k = iota((rows, n), 1)
    first = ((me[0] - (k & 3)) & 3) * (rows // X_DEV) + CAP * (k >> 2)
    g = iota((rows, n), 0)
    live = ((g >= first) & (g < first + lanes)).astype(F32).astype(BF)
    mask = dot(live, jnp.ones((n, 128), BF))
    mask = jnp.concatenate([mask] * 3, axis=1)
    h = jnp.where(mask > 0.5, both[:, :384].astype(F32), 0.0).astype(BF)
    part = dot(h, both[:, 384:], 0, 0)
    last = part[:, 384:]
    sub = iota(last.shape, 0) & 7
    for w in range(3):
        tile = part[:, 128 * w : 128 * w + 128]
        tile = jnp.where(sub == 6, pltpu.roll(last, 6 - w, 0), tile)
        tile = jnp.where(sub == 7, pltpu.roll(last, 4 - w, 0), tile)
        out[:, 128 * w : 128 * w + 128] = tile.astype(BF)


def sum_body(scale, parts, out):
    step = 8 * X_DEV
    total = parts[0:step, :].astype(F32)
    for z in range(1, parts.shape[0] // step):
        total = total + parts[z * step : (z + 1) * step, :].astype(F32)
    total = total / scale
    for x in range(X_DEV):
        for u in range(6):
            v, w = u // 3, u % 3
            out[u, :, 512 * x : 512 * x + 384] = total[8 * x + u : 8 * x + u + 1, :]
            out[u, :, 512 * x + 384 : 512 * x + 512] = total[
                8 * x + 6 + v : 8 * x + 7 + v, 128 * w : 128 * w + 128
            ]


def token_body(routes, residual, returned, out):
    ids = routes[...]
    n = ids.shape[1]
    onehot = (iota((16, n), 0) == ids).astype(F32)
    before = (iota((n, n), 0) < iota((n, n), 1)).astype(BF)
    prefix = dot(onehot.astype(BF), before)
    slot = jnp.sum(onehot * prefix, axis=0, keepdims=True).astype(jnp.int32)
    k = iota((n, n), 0)
    same = (k >> 3) == ids
    pick = (same & ((k & 7) == slot)).astype(BF)
    extra = returned[:, 2048:]
    for r in range(8):
        span = slice(256 * r, 256 * r + 256)
        pick_last = (same & (slot == 8) & ((k & 7) == r)).astype(BF)
        got = dot(pick, returned[:, span], 0, 0) + dot(pick_last, extra, 0, 0)
        out[:, span] = (residual[:, span].astype(F32) + got).astype(BF)


def shards(routes, residual_grad, saved_inputs, saved_preact, expert_grad, w_in, w_out):
    S = jax.ShapeDtypeStruct
    slots, width = saved_inputs.shape[1:]
    units = w_in.shape[1]
    groups = lax.axis_size("z") * lax.axis_size("x")
    me = jnp.stack([lax.axis_index("x"), lax.axis_index("expert")]).astype(jnp.int32)
    ids = routes.reshape(1, 128)
    everyone = lax.all_gather(ids, ("expert", "x"), axis=0, tiled=True)
    hbm = pl.BlockSpec(memory_space=pl.ANY)
    smem = pl.BlockSpec(memory_space=pltpu.SMEM)
    vmem = pl.BlockSpec(memory_space=pltpu.VMEM)
    *sends, slot_grad = call(
        front_body,
        [S((slots, 896), BF)] * X_DEV + [S((128, width + 256), BF)],
        me, expert_grad[0], w_out[0], saved_preact[0], w_in[0], saved_inputs[0],
        flops=8 * slots * units * width,
        limit=63,
        in_specs=[smem] + [hbm] * 5,
        scratch_shapes=[
            pltpu.VMEM((slots, width), BF),
            pltpu.VMEM((units, width), BF),
            pltpu.VMEM((slots, units), BF),
            pltpu.VMEM((units, width), BF),
            pltpu.VMEM((slots, width), BF),
            pltpu.SemaphoreType.DMA((2 * PARTS + 3,)),
        ],
    )
    returned = lax.all_to_all(slot_grad, "expert", split_axis=0, concat_axis=0, tiled=True)
    got = [sends[0]]
    for i in range(1, X_DEV):
        got.append(lax.ppermute(sends[i], "x", [(j, (j + i) % X_DEV) for j in range(X_DEV)]))
    (part,) = call(
        weight_body, [S((8 * groups, 384), BF)], me, *got, everyone,
        flops=2 * 576 * 384 * 512,
        in_specs=[smem] + [vmem] * 5,
    )
    part = lax.all_to_all(part, ("z", "x"), split_axis=0, concat_axis=0, tiled=True)
    (token_grad,) = call(
        token_body, [S((128, width), BF)], ids, residual_grad, returned,
        flops=4 * 128 * 128 * width,
    )
    (grad_in,) = call(
        functools.partial(sum_body, float(groups)), [S((6, 1, width), F32)], part
    )
    return token_grad, jnp.transpose(grad_in, (1, 0, 2))


def solution(mesh):
    fine = Mesh(mesh.devices.reshape(16, 12, X_DEV), ("expert", "z", "x"))
    tokens = P(("expert", "z", "x"), None)
    buffers = P("expert", ("z", "x"), None)
    weights = P("expert", None, None)
    return jax.shard_map(
        shards,
        mesh=fine,
        in_specs=(tokens, tokens, buffers, buffers, buffers, weights, weights),
        out_specs=(tokens, buffers),
        check_vma=False,
    )
```

```python
import functools
import jax
import jax.numpy as jnp
from jax import lax
from jax.experimental import pallas as pl
from jax.experimental.pallas import tpu as pltpu
from jax.sharding import Mesh, PartitionSpec as P

BF = jnp.bfloat16
F32 = jnp.float32
CAP = 9
X_DEV = 4
PARTS = 4
MIB = 1024 * 1024


def iota(shape, axis):
    return lax.broadcasted_iota(jnp.int32, shape, axis)


def dot(a, b, ca=1, cb=0):
    return lax.dot_general(a, b, (((ca,), (cb,)), ((), ())), preferred_element_type=F32)


def call(body, outs, *args, flops=0, limit=32, **more):
    size = sum(a.size * a.dtype.itemsize for a in args) + sum(o.size * o.dtype.itemsize for o in outs)
    return pl.pallas_call(
        body,
        out_shape=outs,
        compiler_params=pltpu.CompilerParams(vmem_limit_bytes=limit * MIB),
        cost_estimate=pl.CostEstimate(flops=flops, bytes_accessed=size, transcendentals=0),
        **more,
    )(*args)


def count_body(routes, out):
    rows = out.shape[0]
    hit = (iota((rows, routes.shape[1]), 0) >> 2) == routes[...]
    total = jnp.sum(hit.astype(F32), axis=1, keepdims=True)
    out[...] = jnp.broadcast_to(total, out.shape).astype(jnp.int32)


def front_body(
    grad, w_out, preact, w_in, inputs,
    send0, send1, send2, send3, slots,
    grad_v, w_out_v, preact_v, w_in_v, spread_v, slots_v, sems,
):
    sends = (send0, send1, send2, send3)
    width = grad.shape[1]
    part = width // PARTS
    loads = []
    for i in range(PARTS):
        span = pl.ds(i * part, part)
        loads.append(pltpu.make_async_copy(grad.at[:, span], grad_v.at[:, span], sems.at[2 * i]))
        loads.append(pltpu.make_async_copy(w_out.at[:, span], w_out_v.at[:, span], sems.at[2 * i + 1]))
    n = 2 * PARTS
    preact_copy = pltpu.make_async_copy(preact, preact_v, sems.at[n])
    w_in_copy = pltpu.make_async_copy(w_in, w_in_v, sems.at[n + 1])
    me = lax.axis_index("x")
    later = []
    for i, send in enumerate(sends):
        first = pl.multiple_of(((me + i) & 3) * 512, 512)
        later.append(
            pltpu.make_async_copy(
                inputs.at[:, pl.ds(first, 512)], send.at[:, pl.ds(384, 512)], sems.at[n + 2 + i]
            )
        )
    for c in loads:
        c.start()
    preact_copy.start()
    w_in_copy.start()
    for c in later:
        c.start()
    rows, units = preact_v.shape
    product = jnp.zeros((rows, units), F32)
    for i in range(PARTS):
        loads[2 * i].wait()
        loads[2 * i + 1].wait()
        span = slice(i * part, i * part + part)
        product = product + dot(grad_v[:, span], w_out_v[:, span], 1, 1)
    preact_copy.wait()
    h = jnp.where(preact_v[...].astype(F32) > 0, product, 0.0).astype(BF)
    col = iota((units, 384), 1)
    place = ((col & 7) < 6) & (iota((units, 384), 0) == 6 * (col >> 3) + (col & 7))
    spread_v[...] = dot(h, place.astype(BF)).astype(BF)
    for i, send in enumerate(sends):
        c = pltpu.make_async_copy(spread_v, send.at[:, pl.ds(0, 384)], sems.at[n + 6 + i])
        c.start()
        later.append(c)
    k = iota((256, rows), 0)
    j = k & 127
    source = CAP * (j >> 3) + jnp.where(k < 128, j & 7, 8)
    picked = dot((iota((256, rows), 1) == source).astype(BF), h).astype(BF)
    w_in_copy.wait()
    row = iota((128, 256), 0) & 7
    last = jnp.zeros((128, 256), F32)
    for r in range(8):
        span = slice(256 * r, 256 * r + 256)
        got = dot(picked, w_in_v[:, span])
        slots_v[:, span] = got[:128].astype(BF)
        last = jnp.where(row == r, got[128:], last)
        if r % 4 == 3:
            half = pl.ds(256 * (r - 3), 1024)
            c = pltpu.make_async_copy(slots_v.at[:, half], slots.at[:, half], sems.at[n + 10 + r // 4])
            c.start()
            later.append(c)
    slots_v[:, width:] = last.astype(BF)
    tail = pl.ds(width, 256)
    c = pltpu.make_async_copy(slots_v.at[:, tail], slots.at[:, tail], sems.at[n + 12])
    c.start()
    later.append(c)
    for c in later:
        c.wait()


def weight_body(own, one, two, three, counts, out):
    both = jnp.concatenate([own[...], one[...], two[...], three[...]], axis=0)
    rows, n = both.shape[0], counts.shape[0]
    eye = (iota((n, n), 0) == iota((n, n), 1)).astype(F32).astype(BF)
    lanes = dot(counts[...].astype(F32).astype(BF), eye, 0, 0)[0:1, :].astype(jnp.int32)
    k = iota((rows, n), 1)
    first = ((lax.axis_index("x") - (k & 3)) & 3) * (rows // X_DEV) + CAP * (k >> 2)
    g = iota((rows, n), 0)
    live = ((g >= first) & (g < first + lanes)).astype(F32).astype(BF)
    mask = dot(live, jnp.ones((n, 128), BF)).astype(BF)
    h = both[:, :384] * jnp.concatenate([mask] * 3, axis=1)
    part = dot(h, both[:, 384:], 0, 0)
    last = part[:, 384:]
    sub = iota(last.shape, 0) & 7
    for w in range(3):
        tile = part[:, 128 * w : 128 * w + 128]
        tile = jnp.where(sub == 6, pltpu.roll(last, 6 - w, 0), tile)
        tile = jnp.where(sub == 7, pltpu.roll(last, 4 - w, 0), tile)
        out[:, 128 * w : 128 * w + 128] = tile.astype(BF)


def sum_body(scale, parts, out):
    step = 8 * X_DEV
    total = parts[0:step, :].astype(F32)
    for z in range(1, parts.shape[0] // step):
        total = total + parts[z * step : (z + 1) * step, :].astype(F32)
    total = total / scale
    for x in range(X_DEV):
        for u in range(6):
            v, w = u // 3, u % 3
            out[u, :, 512 * x : 512 * x + 384] = total[8 * x + u : 8 * x + u + 1, :]
            out[u, :, 512 * x + 384 : 512 * x + 512] = total[
                8 * x + 6 + v : 8 * x + 7 + v, 128 * w : 128 * w + 128
            ]


def token_body(routes, residual, returned, out):
    ids = routes[...]
    n = ids.shape[1]
    onehot = (iota((16, n), 0) == ids).astype(F32)
    before = (iota((n, n), 0) < iota((n, n), 1)).astype(BF)
    prefix = dot(onehot.astype(BF), before)
    slot = jnp.sum(onehot * prefix, axis=0, keepdims=True).astype(jnp.int32)
    k = iota((n, n), 0)
    same = (k >> 3) == ids
    pick = (same & ((k & 7) == slot)).astype(BF)
    extra = returned[:, 2048:]
    for r in range(8):
        span = slice(256 * r, 256 * r + 256)
        pick_last = (same & (slot == 8) & ((k & 7) == r)).astype(BF)
        got = dot(pick, returned[:, span], 0, 0) + dot(pick_last, extra, 0, 0)
        out[:, span] = (residual[:, span].astype(F32) + got).astype(BF)


def shards(routes, residual_grad, saved_inputs, saved_preact, expert_grad, w_in, w_out):
    S = jax.ShapeDtypeStruct
    slots, width = saved_inputs.shape[1:]
    units = w_in.shape[1]
    groups = lax.axis_size("z") * lax.axis_size("x")
    ids = routes.reshape(1, 128)
    hbm = pl.BlockSpec(memory_space=pl.ANY)
    (counts,) = call(count_body, [S((64, 128), jnp.int32)], ids, limit=63)
    counts = lax.all_to_all(
        counts.reshape(64, 1, 128), ("expert", "x"), split_axis=0, concat_axis=0, tiled=True
    ).reshape(64, 128)
    *sends, slot_grad = call(
        front_body,
        [S((slots, 896), BF)] * X_DEV + [S((128, width + 256), BF)],
        expert_grad[0], w_out[0], saved_preact[0], w_in[0], saved_inputs[0],
        flops=8 * slots * units * width,
        limit=63,
        in_specs=[hbm] * 5,
        out_specs=[hbm] * 5,
        scratch_shapes=[
            pltpu.VMEM((slots, width), BF),
            pltpu.VMEM((units, width), BF),
            pltpu.VMEM((slots, units), BF),
            pltpu.VMEM((units, width), BF),
            pltpu.VMEM((slots, 384), BF),
            pltpu.VMEM((128, width + 256), BF),
            pltpu.SemaphoreType.DMA((2 * PARTS + 13,)),
        ],
    )
    returned = lax.all_to_all(slot_grad, "expert", split_axis=0, concat_axis=0, tiled=True)
    got = [sends[0]]
    for i in range(1, X_DEV):
        got.append(lax.ppermute(sends[i], "x", [(j, (j + i) % X_DEV) for j in range(X_DEV)]))
    (part,) = call(
        weight_body, [S((8 * groups, 384), BF)], *got, counts,
        flops=2 * 576 * 384 * 512,
    )
    part = lax.all_to_all(part, ("z", "x"), split_axis=0, concat_axis=0, tiled=True)
    (token_grad,) = call(
        token_body, [S((128, width), BF)], ids, residual_grad, returned,
        flops=4 * 128 * 128 * width,
    )
    (grad_in,) = call(
        functools.partial(sum_body, float(groups)), [S((6, 1, width), F32)], part
    )
    return token_grad, jnp.transpose(grad_in, (1, 0, 2))


def solution(mesh):
    fine = Mesh(mesh.devices.reshape(16, 12, X_DEV), ("expert", "z", "x"))
    tokens = P(("expert", "z", "x"), None)
    buffers = P("expert", ("z", "x"), None)
    weights = P("expert", None, None)
    return jax.shard_map(
        shards,
        mesh=fine,
        in_specs=(tokens, tokens, buffers, buffers, buffers, weights, weights),
        out_specs=(tokens, buffers),
        check_vma=False,
    )
```

```python
import functools
import jax
import jax.numpy as jnp
from jax import lax
from jax.experimental import pallas as pl
from jax.experimental.pallas import tpu as pltpu
from jax.sharding import Mesh, PartitionSpec as P

BF = jnp.bfloat16
F32 = jnp.float32
CAP = 9
X_DEV = 4
Z_DEV = 12
PARTS = 4
MIB = 1024 * 1024


def iota(shape, axis):
    return lax.broadcasted_iota(jnp.int32, shape, axis)


def as_bf(mask):
    return mask.astype(F32).astype(BF)


def dot(a, b, ca=1, cb=0):
    return lax.dot_general(a, b, (((ca,), (cb,)), ((), ())), preferred_element_type=F32)


def call(body, outs, *args, flops=0, limit=32, **more):
    size = sum(a.size * a.dtype.itemsize for a in args) + sum(o.size * o.dtype.itemsize for o in outs)
    return pl.pallas_call(
        body,
        out_shape=outs,
        compiler_params=pltpu.CompilerParams(vmem_limit_bytes=limit * MIB),
        cost_estimate=pl.CostEstimate(flops=flops, bytes_accessed=size, transcendentals=0),
        **more,
    )(*args)


def count_body(routes, out):
    hit = iota((out.shape[0], routes.shape[1]), 0) == routes[...]
    total = jnp.sum(hit.astype(F32), axis=1, keepdims=True)
    out[...] = jnp.broadcast_to(total, out.shape).astype(jnp.int32)


def front_body(
    grad, w_out, preact, w_in, hidden, slots,
    grad_v, w_out_v, preact_v, w_in_v, slots_v, sems,
):
    width = grad.shape[1]
    part = width // PARTS
    loads = []
    for i in range(PARTS):
        span = pl.ds(i * part, part)
        loads.append(pltpu.make_async_copy(grad.at[:, span], grad_v.at[:, span], sems.at[2 * i]))
        loads.append(pltpu.make_async_copy(w_out.at[:, span], w_out_v.at[:, span], sems.at[2 * i + 1]))
    n = 2 * PARTS
    preact_copy = pltpu.make_async_copy(preact, preact_v, sems.at[n])
    w_in_copy = pltpu.make_async_copy(w_in, w_in_v, sems.at[n + 1])
    for c in loads:
        c.start()
    preact_copy.start()
    w_in_copy.start()
    rows, units = preact_v.shape
    product = jnp.zeros((rows, units), F32)
    for i in range(PARTS):
        loads[2 * i].wait()
        loads[2 * i + 1].wait()
        span = slice(i * part, i * part + part)
        product = product + dot(grad_v[:, span], w_out_v[:, span], 1, 1)
    preact_copy.wait()
    h = jnp.where(preact_v[...].astype(F32) > 0, product, 0.0).astype(BF)
    hidden[...] = h
    k = iota((256, rows), 0)
    j = k & 127
    source = CAP * (j >> 3) + jnp.where(k < 128, j & 7, 8)
    picked = dot(as_bf(iota((256, rows), 1) == source), h).astype(BF)
    w_in_copy.wait()
    row = iota((128, 256), 0) & 7
    last = jnp.zeros((128, 256), F32)
    stores = []
    for r in range(8):
        span = slice(256 * r, 256 * r + 256)
        got = dot(picked, w_in_v[:, span])
        slots_v[:, span] = got[:128].astype(BF)
        last = jnp.where(row == r, got[128:], last)
        if r % 4 == 3:
            half = pl.ds(256 * (r - 3), 1024)
            stores.append(
                pltpu.make_async_copy(slots_v.at[:, half], slots.at[:, half], sems.at[n + 2 + r // 4])
            )
            stores[-1].start()
    slots_v[:, width:] = last.astype(BF)
    tail = pl.ds(width, 256)
    stores.append(pltpu.make_async_copy(slots_v.at[:, tail], slots.at[:, tail], sems.at[n + 4]))
    stores[-1].start()
    for c in stores:
        c.wait()


def weight_body(hidden, inputs, counts, *outs):
    rows, units = hidden.shape
    j = iota((96, units), 0)
    unit = iota((96, units), 1)
    n = counts.shape[0]
    g = iota((n, rows), 1)
    first = CAP * iota((n, rows), 0)
    live = (g >= first) & (g < first + counts[:, :1])
    mask = as_bf(jnp.sum(live.astype(F32), axis=0, keepdims=True) > 0.5)
    me = lax.axis_index("x")
    for k, out in enumerate(outs):
        owner = X_DEV * (j >> 3) + ((me + k) & 3)
        place = ((j & 7) < 6) & (unit == 6 * owner + (j & 7))
        spread = dot(as_bf(place), hidden[...], 1, 1).astype(BF) * mask
        last = dot(spread, inputs[:, 1536:])
        sub = iota(last.shape, 0) & 7
        for w in range(3):
            span = slice(512 * w, 512 * w + 512)
            tile = dot(spread, inputs[:, span])
            tile = jnp.where(sub == 6, pltpu.roll(last, 6 - w, 0), tile)
            tile = jnp.where(sub == 7, pltpu.roll(last, 4 - w, 0), tile)
            out[:, span] = tile.astype(BF)


def add_body(own, one, two, three, out):
    total = (own[...].astype(F32) + one[...].astype(F32)) + (two[...].astype(F32) + three[...].astype(F32))
    out[...] = total.astype(BF)


def sum_body(scale, parts, out):
    total = parts[0:8, :].astype(F32)
    for z in range(1, parts.shape[0] // 8):
        total = total + parts[8 * z : 8 * z + 8, :].astype(F32)
    total = total / scale
    for u in range(6):
        v, w = u // 3, u % 3
        out[u, :, :1536] = total[u : u + 1, :]
        out[u, :, 1536:] = total[6 + v : 7 + v, 512 * w : 512 * w + 512]


def token_body(routes, residual, returned, out):
    ids = routes[...]
    n = ids.shape[1]
    onehot = (iota((16, n), 0) == ids).astype(F32)
    before = as_bf(iota((n, n), 0) < iota((n, n), 1))
    prefix = dot(onehot.astype(BF), before)
    slot = jnp.sum(onehot * prefix, axis=0, keepdims=True).astype(jnp.int32)
    k = iota((n, n), 0)
    same = (k >> 3) == ids
    pick = as_bf(same & ((k & 7) == slot))
    extra = returned[:, 2048:]
    for r in range(8):
        span = slice(256 * r, 256 * r + 256)
        pick_last = as_bf(same & (slot == 8) & ((k & 7) == r))
        got = dot(pick, returned[:, span], 0, 0) + dot(pick_last, extra, 0, 0)
        out[:, span] = (residual[:, span].astype(F32) + got).astype(BF)


def shards(routes, residual_grad, saved_inputs, saved_preact, expert_grad, w_in, w_out):
    S = jax.ShapeDtypeStruct
    slots, width = saved_inputs.shape[1:]
    units = w_in.shape[1]
    groups = lax.axis_size("z") * lax.axis_size("x")
    ids = routes.reshape(1, 128)
    hbm = pl.BlockSpec(memory_space=pl.ANY)
    vmem = pl.BlockSpec(memory_space=pltpu.VMEM)
    (counts,) = call(count_body, [S((16, 128), jnp.int32)], ids, limit=63)
    counts = lax.all_to_all(
        counts.reshape(16, 1, 128), "expert", split_axis=0, concat_axis=0, tiled=True
    ).reshape(16, 128)
    hidden, slot_grad = call(
        front_body,
        [S((slots, units), BF), S((128, width + 256), BF)],
        expert_grad[0], w_out[0], saved_preact[0], w_in[0],
        flops=6 * slots * units * width,
        limit=63,
        in_specs=[hbm] * 4,
        out_specs=[vmem, hbm],
        scratch_shapes=[
            pltpu.VMEM((slots, width), BF),
            pltpu.VMEM((units, width), BF),
            pltpu.VMEM((slots, units), BF),
            pltpu.VMEM((units, width), BF),
            pltpu.VMEM((128, width + 256), BF),
            pltpu.SemaphoreType.DMA((2 * PARTS + 5,)),
        ],
    )
    returned = lax.all_to_all(slot_grad, "expert", split_axis=0, concat_axis=0, tiled=True)
    sends = call(
        weight_body, [S((8 * Z_DEV, 1536), BF)] * X_DEV, hidden, saved_inputs[0], counts,
        flops=2 * slots * 384 * width,
    )
    got = [sends[0]]
    for i in range(1, X_DEV):
        got.append(lax.ppermute(sends[i], "x", [(j, (j + i) % X_DEV) for j in range(X_DEV)]))
    (part,) = call(add_body, [S((8 * Z_DEV, 1536), BF)], *got)
    part = lax.all_to_all(part, "z", split_axis=0, concat_axis=0, tiled=True)
    (token_grad,) = call(
        token_body, [S((128, width), BF)], ids, residual_grad, returned,
        flops=4 * 128 * 128 * width,
    )
    (grad_in,) = call(
        functools.partial(sum_body, float(groups)), [S((6, 1, width), F32)], part
    )
    return token_grad, jnp.transpose(grad_in, (1, 0, 2))


def solution(mesh):
    fine = Mesh(mesh.devices.reshape(16, Z_DEV, X_DEV), ("expert", "z", "x"))
    tokens = P(("expert", "z", "x"), None)
    buffers = P("expert", ("z", "x"), None)
    weights = P("expert", None, None)
    return jax.shard_map(
        shards,
        mesh=fine,
        in_specs=(tokens, tokens, buffers, buffers, buffers, weights, weights),
        out_specs=(tokens, buffers),
        check_vma=False,
    )
```

```python
import functools
import jax
import jax.numpy as jnp
from jax import lax
from jax.experimental import pallas as pl
from jax.experimental.pallas import tpu as pltpu
from jax.sharding import Mesh, PartitionSpec as P

BF = jnp.bfloat16
F32 = jnp.float32
CAP = 9
X_DEV = 4
Z_DEV = 12
PARTS = 4
MIB = 1024 * 1024


def iota(shape, axis):
    return lax.broadcasted_iota(jnp.int32, shape, axis)


def as_bf(mask):
    return mask.astype(F32).astype(BF)


def dot(a, b, ca=1, cb=0):
    return lax.dot_general(a, b, (((ca,), (cb,)), ((), ())), preferred_element_type=F32)


def call(body, outs, *args, flops=0, limit=32, **more):
    size = sum(a.size * a.dtype.itemsize for a in args) + sum(o.size * o.dtype.itemsize for o in outs)
    return pl.pallas_call(
        body,
        out_shape=outs,
        compiler_params=pltpu.CompilerParams(vmem_limit_bytes=limit * MIB),
        cost_estimate=pl.CostEstimate(flops=flops, bytes_accessed=size, transcendentals=0),
        **more,
    )(*args)


def front_body(
    grad, w_out, preact, w_in, hidden, slots,
    grad_v, w_out_v, preact_v, w_in_v, slots_v, sems,
):
    width = grad.shape[1]
    part = width // PARTS
    loads = []
    for i in range(PARTS):
        span = pl.ds(i * part, part)
        loads.append(pltpu.make_async_copy(grad.at[:, span], grad_v.at[:, span], sems.at[2 * i]))
        loads.append(pltpu.make_async_copy(w_out.at[:, span], w_out_v.at[:, span], sems.at[2 * i + 1]))
    n = 2 * PARTS
    preact_copy = pltpu.make_async_copy(preact, preact_v, sems.at[n])
    w_in_copy = pltpu.make_async_copy(w_in, w_in_v, sems.at[n + 1])
    for c in loads:
        c.start()
    preact_copy.start()
    w_in_copy.start()
    rows, units = preact_v.shape
    product = jnp.zeros((rows, units), F32)
    for i in range(PARTS):
        loads[2 * i].wait()
        loads[2 * i + 1].wait()
        span = slice(i * part, i * part + part)
        product = product + dot(grad_v[:, span], w_out_v[:, span], 1, 1)
    preact_copy.wait()
    h = jnp.where(preact_v[...].astype(F32) > 0, product, 0.0).astype(BF)
    hidden[...] = h
    k = iota((256, rows), 0)
    j = k & 127
    block = 2 * (j >> 4) + (((j >> 3) & 1) ^ lax.axis_index("core"))
    source = CAP * block + jnp.where(k < 128, j & 7, 8)
    picked = dot(as_bf(iota((256, rows), 1) == source), h).astype(BF)
    w_in_copy.wait()
    row = iota((128, 256), 0) & 7
    last = jnp.zeros((128, 256), F32)
    stores = []
    for r in range(8):
        span = slice(256 * r, 256 * r + 256)
        got = dot(picked, w_in_v[:, span])
        slots_v[:, span] = got[:128].astype(BF)
        last = jnp.where(row == r, got[128:], last)
        if r % 4 == 3:
            half = pl.ds(256 * (r - 3), 1024)
            stores.append(
                pltpu.make_async_copy(slots_v.at[:, half], slots.at[:, half], sems.at[n + 2 + r // 4])
            )
            stores[-1].start()
    slots_v[:, width:] = last.astype(BF)
    tail = pl.ds(width, 256)
    stores.append(pltpu.make_async_copy(slots_v.at[:, tail], slots.at[:, tail], sems.at[n + 4]))
    stores[-1].start()
    for c in stores:
        c.wait()


def weight_body(hidden, inputs, routes, *outs):
    rows, units = hidden.shape
    expert = 2 * lax.axis_index("y") + lax.axis_index("core")
    counts = jnp.sum((routes[...] == expert).astype(F32), axis=1, keepdims=True).astype(jnp.int32)
    j = iota((96, units), 0)
    unit = iota((96, units), 1)
    n = routes.shape[0]
    g = iota((n, rows), 1)
    first = CAP * iota((n, rows), 0)
    live = (g >= first) & (g < first + counts)
    mask = as_bf(jnp.sum(live.astype(F32), axis=0, keepdims=True) > 0.5)
    me = lax.axis_index("x")
    for k, out in enumerate(outs):
        owner = X_DEV * (j >> 3) + ((me + k) & 3)
        place = ((j & 7) < 6) & (unit == 6 * owner + (j & 7))
        spread = dot(as_bf(place), hidden[...], 1, 1).astype(BF) * mask
        last = dot(spread, inputs[:, 1536:])
        sub = iota(last.shape, 0) & 7
        for w in range(3):
            span = slice(512 * w, 512 * w + 512)
            tile = dot(spread, inputs[:, span])
            tile = jnp.where(sub == 6, pltpu.roll(last, 6 - w, 0), tile)
            tile = jnp.where(sub == 7, pltpu.roll(last, 4 - w, 0), tile)
            out[:, span] = tile.astype(BF)


def add_body(own, one, two, three, out):
    total = (own[...].astype(F32) + one[...].astype(F32)) + (two[...].astype(F32) + three[...].astype(F32))
    out[...] = total.astype(BF)


def sum_body(scale, parts, out):
    total = parts[0:8, :].astype(F32)
    for z in range(1, parts.shape[0] // 8):
        total = total + parts[8 * z : 8 * z + 8, :].astype(F32)
    total = total / scale
    for u in range(6):
        v, w = u // 3, u % 3
        out[u, :, :1536] = total[u : u + 1, :]
        out[u, :, 1536:] = total[6 + v : 7 + v, 512 * w : 512 * w + 512]


def token_body(routes, residual, near, far, out):
    ids = routes[...]
    n = ids.shape[1]
    onehot = (iota((16, n), 0) == ids).astype(F32)
    before = as_bf(iota((n, n), 0) < iota((n, n), 1))
    prefix = dot(onehot.astype(BF), before)
    slot = jnp.sum(onehot * prefix, axis=0, keepdims=True).astype(jnp.int32)
    here = (ids & 1) == lax.axis_index("core")
    k = iota((near.shape[0], n), 0)
    same_near = here & ((k >> 3) == 2 * (ids >> 1))
    c_near = k & 7
    k = iota((far.shape[0], n), 0)
    same_far = jnp.logical_not(here) & ((k >> 3) == (ids >> 1))
    c_far = k & 7
    pick_near = as_bf(same_near & (c_near == slot))
    pick_far = as_bf(same_far & (c_far == slot))
    last_near = near[:, 2048:]
    last_far = far[:, 2048:]
    for r in range(8):
        span = slice(256 * r, 256 * r + 256)
        tail_near = as_bf(same_near & (slot == 8) & (c_near == r))
        tail_far = as_bf(same_far & (slot == 8) & (c_far == r))
        got = dot(pick_near, near[:, span], 0, 0) + dot(pick_far, far[:, span], 0, 0)
        got = got + dot(tail_near, last_near, 0, 0) + dot(tail_far, last_far, 0, 0)
        out[:, span] = (residual[:, span].astype(F32) + got).astype(BF)


def shards(routes, residual_grad, saved_inputs, saved_preact, expert_grad, w_in, w_out):
    S = jax.ShapeDtypeStruct
    slots, width = saved_inputs.shape[1:]
    units = w_in.shape[1]
    groups = lax.axis_size("z") * lax.axis_size("x")
    ids = routes.reshape(1, 128)
    hbm = pl.BlockSpec(memory_space=pl.ANY)
    vmem = pl.BlockSpec(memory_space=pltpu.VMEM)
    experts = ("y", "core")
    everyone = lax.all_to_all(
        jnp.broadcast_to(ids[:, None], (16, 1, 128)), experts, split_axis=0, concat_axis=0, tiled=True
    ).reshape(16, 128)
    hidden, slot_grad = call(
        front_body,
        [S((slots, units), BF), S((128, width + 256), BF)],
        expert_grad[0], w_out[0], saved_preact[0], w_in[0],
        flops=6 * slots * units * width,
        limit=63,
        in_specs=[hbm] * 4,
        out_specs=[vmem, hbm],
        scratch_shapes=[
            pltpu.VMEM((slots, width), BF),
            pltpu.VMEM((units, width), BF),
            pltpu.VMEM((slots, units), BF),
            pltpu.VMEM((units, width), BF),
            pltpu.VMEM((128, width + 256), BF),
            pltpu.SemaphoreType.DMA((2 * PARTS + 5,)),
        ],
    )
    sends = call(
        weight_body, [S((8 * Z_DEV, 1536), BF)] * X_DEV, hidden, saved_inputs[0], everyone,
        flops=2 * slots * 384 * width,
    )
    *sends, slot_grad = lax.optimization_barrier((*sends, slot_grad))
    near = lax.all_to_all(slot_grad, "y", split_axis=0, concat_axis=0, tiled=True)
    far = near.reshape(8, 2, 8, width + 256)[:, 1].reshape(64, width + 256)
    far = lax.ppermute(far, "core", [(0, 1), (1, 0)])
    got = [sends[0]]
    for i in (2, 1, 3):
        got.append(lax.ppermute(sends[i], "x", [(j, (j + i) % X_DEV) for j in range(X_DEV)]))
    (part,) = call(add_body, [S((8 * Z_DEV, 1536), BF)], *got)
    part = lax.all_to_all(part, "z", split_axis=0, concat_axis=0, tiled=True)
    (token_grad,) = call(
        token_body, [S((128, width), BF)], ids, residual_grad, near, far,
        flops=6 * 128 * 128 * width,
    )
    token_grad, part = lax.optimization_barrier((token_grad, part))
    (grad_in,) = call(
        functools.partial(sum_body, float(groups)), [S((6, 1, width), F32)], part
    )
    return token_grad, jnp.transpose(grad_in, (1, 0, 2))


def solution(mesh):
    fine = Mesh(mesh.devices.reshape(8, 2, Z_DEV, X_DEV), ("y", "core", "z", "x"))
    tokens = P(("y", "core", "z", "x"), None)
    buffers = P(("y", "core"), ("z", "x"), None)
    weights = P(("y", "core"), None, None)
    return jax.shard_map(
        shards,
        mesh=fine,
        in_specs=(tokens, tokens, buffers, buffers, buffers, weights, weights),
        out_specs=(tokens, buffers),
        check_vma=False,
    )
```

```python
import functools
import jax
import jax.numpy as jnp
from jax import lax
from jax.experimental import pallas as pl
from jax.experimental.pallas import tpu as pltpu
from jax.sharding import Mesh, PartitionSpec as P

BF = jnp.bfloat16
F32 = jnp.float32
CAP = 9
X_DEV = 4
Z_DEV = 12
PARTS = 4
MIB = 1024 * 1024


def iota(shape, axis):
    return lax.broadcasted_iota(jnp.int32, shape, axis)


def as_bf(mask):
    return mask.astype(F32).astype(BF)


def dot(a, b, ca=1, cb=0):
    return lax.dot_general(a, b, (((ca,), (cb,)), ((), ())), preferred_element_type=F32)


def call(body, outs, *args, flops=0, limit=32, **more):
    size = sum(a.size * a.dtype.itemsize for a in args) + sum(o.size * o.dtype.itemsize for o in outs)
    return pl.pallas_call(
        body,
        out_shape=outs,
        compiler_params=pltpu.CompilerParams(vmem_limit_bytes=limit * MIB),
        cost_estimate=pl.CostEstimate(flops=flops, bytes_accessed=size, transcendentals=0),
        **more,
    )(*args)


def front_body(
    grad, w_out, preact, w_in, hidden, slots,
    grad_v, w_out_v, preact_v, w_in_v, slots_v, sems,
):
    width = grad.shape[1]
    part = width // PARTS
    loads = []
    for i in range(PARTS):
        span = pl.ds(i * part, part)
        loads.append(pltpu.make_async_copy(grad.at[:, span], grad_v.at[:, span], sems.at[2 * i]))
        loads.append(pltpu.make_async_copy(w_out.at[:, span], w_out_v.at[:, span], sems.at[2 * i + 1]))
    n = 2 * PARTS
    preact_copy = pltpu.make_async_copy(preact, preact_v, sems.at[n])
    w_in_copy = pltpu.make_async_copy(w_in, w_in_v, sems.at[n + 1])
    for c in loads:
        c.start()
    preact_copy.start()
    w_in_copy.start()
    rows, units = preact_v.shape
    product = jnp.zeros((rows, units), F32)
    for i in range(PARTS):
        loads[2 * i].wait()
        loads[2 * i + 1].wait()
        span = slice(i * part, i * part + part)
        product = product + dot(grad_v[:, span], w_out_v[:, span], 1, 1)
    preact_copy.wait()
    h = jnp.where(preact_v[...].astype(F32) > 0, product, 0.0).astype(BF)
    hidden[...] = h
    k = iota((256, rows), 0)
    j = k & 127
    block = 2 * (j >> 4) + (((j >> 3) & 1) ^ lax.axis_index("core"))
    source = CAP * block + jnp.where(k < 128, j & 7, 8)
    picked = dot(as_bf(iota((256, rows), 1) == source), h).astype(BF)
    w_in_copy.wait()
    row = iota((128, 256), 0) & 7
    last = jnp.zeros((128, 256), F32)
    stores = []
    for r in range(8):
        span = slice(256 * r, 256 * r + 256)
        got = dot(picked, w_in_v[:, span])
        slots_v[:, span] = got[:128].astype(BF)
        last = jnp.where(row == r, got[128:], last)
        if r % 4 == 3:
            half = pl.ds(256 * (r - 3), 1024)
            stores.append(
                pltpu.make_async_copy(slots_v.at[:, half], slots.at[:, half], sems.at[n + 2 + r // 4])
            )
            stores[-1].start()
    slots_v[:, width:] = last.astype(BF)
    tail = pl.ds(width, 256)
    stores.append(pltpu.make_async_copy(slots_v.at[:, tail], slots.at[:, tail], sems.at[n + 4]))
    stores[-1].start()
    for c in stores:
        c.wait()


def weight_body(hidden, inputs, routes, *outs):
    rows, units = hidden.shape
    expert = 2 * lax.axis_index("y") + lax.axis_index("core")
    counts = jnp.sum((routes[...] == expert).astype(F32), axis=1, keepdims=True).astype(jnp.int32)
    j = iota((96, units), 0)
    unit = iota((96, units), 1)
    n = routes.shape[0]
    g = iota((n, rows), 1)
    first = CAP * iota((n, rows), 0)
    live = (g >= first) & (g < first + counts)
    mask = as_bf(jnp.sum(live.astype(F32), axis=0, keepdims=True) > 0.5)
    for k, out in enumerate(outs):
        z = 2 * (j >> 4) + (lax.axis_index("zl") ^ (k >> 1))
        x = 2 * ((j >> 3) & 1) + (lax.axis_index("xl") ^ (k & 1))
        owner = X_DEV * z + x
        place = ((j & 7) < 6) & (unit == 6 * owner + (j & 7))
        spread = dot(as_bf(place), hidden[...], 1, 1).astype(BF) * mask
        last = dot(spread, inputs[:, 1536:])
        sub = iota(last.shape, 0) & 7
        for w in range(3):
            span = slice(512 * w, 512 * w + 512)
            tile = dot(spread, inputs[:, span])
            tile = jnp.where(sub == 6, pltpu.roll(last, 6 - w, 0), tile)
            tile = jnp.where(sub == 7, pltpu.roll(last, 4 - w, 0), tile)
            out[:, span] = tile.astype(BF)


def add_body(own, one, two, three, out):
    total = (own[...].astype(F32) + one[...].astype(F32)) + (two[...].astype(F32) + three[...].astype(F32))
    out[...] = total.astype(BF)


def sum_body(scale, parts, out):
    total = parts[0:8, :].astype(F32)
    for z in range(1, parts.shape[0] // 8):
        total = total + parts[8 * z : 8 * z + 8, :].astype(F32)
    total = total / scale
    for u in range(6):
        v, w = u // 3, u % 3
        out[u, :, :1536] = total[u : u + 1, :]
        out[u, :, 1536:] = total[6 + v : 7 + v, 512 * w : 512 * w + 512]


def token_body(routes, residual, near, far, out):
    ids = routes[...]
    n = ids.shape[1]
    onehot = (iota((16, n), 0) == ids).astype(F32)
    before = as_bf(iota((n, n), 0) < iota((n, n), 1))
    prefix = dot(onehot.astype(BF), before)
    slot = jnp.sum(onehot * prefix, axis=0, keepdims=True).astype(jnp.int32)
    here = (ids & 1) == lax.axis_index("core")
    k = iota((near.shape[0], n), 0)
    same_near = here & ((k >> 3) == 2 * (ids >> 1))
    c_near = k & 7
    k = iota((far.shape[0], n), 0)
    same_far = jnp.logical_not(here) & ((k >> 3) == (ids >> 1))
    c_far = k & 7
    pick_near = as_bf(same_near & (c_near == slot))
    pick_far = as_bf(same_far & (c_far == slot))
    last_near = near[:, 2048:]
    last_far = far[:, 2048:]
    for r in range(8):
        span = slice(256 * r, 256 * r + 256)
        tail_near = as_bf(same_near & (slot == 8) & (c_near == r))
        tail_far = as_bf(same_far & (slot == 8) & (c_far == r))
        got = dot(pick_near, near[:, span], 0, 0) + dot(pick_far, far[:, span], 0, 0)
        got = got + dot(tail_near, last_near, 0, 0) + dot(tail_far, last_far, 0, 0)
        out[:, span] = (residual[:, span].astype(F32) + got).astype(BF)


def shards(routes, residual_grad, saved_inputs, saved_preact, expert_grad, w_in, w_out):
    S = jax.ShapeDtypeStruct
    slots, width = saved_inputs.shape[1:]
    units = w_in.shape[1]
    groups = Z_DEV * X_DEV
    ids = routes.reshape(1, 128)
    hbm = pl.BlockSpec(memory_space=pl.ANY)
    vmem = pl.BlockSpec(memory_space=pltpu.VMEM)
    experts = ("y", "core")
    everyone = lax.all_to_all(
        jnp.broadcast_to(ids[:, None], (16, 1, 128)), experts, split_axis=0, concat_axis=0, tiled=True
    ).reshape(16, 128)
    hidden, slot_grad = call(
        front_body,
        [S((slots, units), BF), S((128, width + 256), BF)],
        expert_grad[0], w_out[0], saved_preact[0], w_in[0],
        flops=6 * slots * units * width,
        limit=63,
        in_specs=[hbm] * 4,
        out_specs=[vmem, hbm],
        scratch_shapes=[
            pltpu.VMEM((slots, width), BF),
            pltpu.VMEM((units, width), BF),
            pltpu.VMEM((slots, units), BF),
            pltpu.VMEM((units, width), BF),
            pltpu.VMEM((128, width + 256), BF),
            pltpu.SemaphoreType.DMA((2 * PARTS + 5,)),
        ],
    )
    sends = call(
        weight_body, [S((96, 1536), BF)] * 4, hidden, saved_inputs[0], everyone,
        flops=2 * slots * 384 * width,
    )
    *sends, slot_grad = lax.optimization_barrier((*sends, slot_grad))
    near = lax.all_to_all(slot_grad, "y", split_axis=0, concat_axis=0, tiled=True)
    far = near.reshape(8, 2, 8, width + 256)[:, 1].reshape(64, width + 256)
    far = lax.ppermute(far, "core", [(0, 1), (1, 0)])
    both = ("zl", "xl")
    got = [lax.ppermute(sends[3], both, [(0, 3), (1, 2), (2, 1), (3, 0)])]
    got.append(lax.ppermute(sends[2], "zl", [(0, 1), (1, 0)]))
    got.append(lax.ppermute(sends[1], "xl", [(0, 1), (1, 0)]))
    (part,) = call(add_body, [S((96, 1536), BF)], sends[0], *got)
    part = lax.all_to_all(part, ("zh", "xh"), split_axis=0, concat_axis=0, tiled=True)
    (token_grad,) = call(
        token_body, [S((128, width), BF)], ids, residual_grad, near, far,
        flops=6 * 128 * 128 * width,
    )
    token_grad, part = lax.optimization_barrier((token_grad, part))
    (grad_in,) = call(
        functools.partial(sum_body, float(groups)), [S((6, 1, width), F32)], part
    )
    return token_grad, jnp.transpose(grad_in, (1, 0, 2))


def solution(mesh):
    fine = Mesh(mesh.devices.reshape(8, 2, 6, 2, 2, 2), ("y", "core", "zh", "zl", "xh", "xl"))
    dp = ("zh", "zl", "xh", "xl")
    tokens = P(("y", "core", *dp), None)
    buffers = P(("y", "core"), dp, None)
    weights = P(("y", "core"), None, None)
    return jax.shard_map(
        shards,
        mesh=fine,
        in_specs=(tokens, tokens, buffers, buffers, buffers, weights, weights),
        out_specs=(tokens, buffers),
        check_vma=False,
    )
```

```python
import functools
import jax
import jax.numpy as jnp
from jax import lax
from jax.experimental import pallas as pl
from jax.experimental.pallas import tpu as pltpu
from jax.sharding import Mesh, PartitionSpec as P

BF = jnp.bfloat16
F32 = jnp.float32
CAP = 9
X_DEV = 4
Z_DEV = 12
PARTS = 4
MIB = 1024 * 1024


def iota(shape, axis):
    return lax.broadcasted_iota(jnp.int32, shape, axis)


def as_bf(mask):
    return mask.astype(F32).astype(BF)


def dot(a, b, ca=1, cb=0):
    return lax.dot_general(a, b, (((ca,), (cb,)), ((), ())), preferred_element_type=F32)


def call(body, outs, *args, flops=0, limit=32, **more):
    size = sum(a.size * a.dtype.itemsize for a in args) + sum(o.size * o.dtype.itemsize for o in outs)
    return pl.pallas_call(
        body,
        out_shape=outs,
        compiler_params=pltpu.CompilerParams(vmem_limit_bytes=limit * MIB),
        cost_estimate=pl.CostEstimate(flops=flops, bytes_accessed=size, transcendentals=0),
        **more,
    )(*args)


def hidden_body(grad, w_out, preact, hidden, grad_v, w_out_v, preact_v, sems):
    width = grad.shape[1]
    part = width // PARTS
    loads = []
    for i in range(PARTS):
        span = pl.ds(i * part, part)
        loads.append(pltpu.make_async_copy(grad.at[:, span], grad_v.at[:, span], sems.at[2 * i]))
        loads.append(pltpu.make_async_copy(w_out.at[:, span], w_out_v.at[:, span], sems.at[2 * i + 1]))
    preact_copy = pltpu.make_async_copy(preact, preact_v, sems.at[2 * PARTS])
    for c in loads:
        c.start()
    preact_copy.start()
    product = jnp.zeros(hidden.shape, F32)
    for i in range(PARTS):
        loads[2 * i].wait()
        loads[2 * i + 1].wait()
        span = slice(i * part, i * part + part)
        product = product + dot(grad_v[:, span], w_out_v[:, span], 1, 1)
    preact_copy.wait()
    hidden[...] = jnp.where(preact_v[...].astype(F32) > 0, product, 0.0).astype(BF)


def slot_body(hidden, w_in, *outs):
    rows = hidden.shape[0]
    width = w_in.shape[1]
    k = iota((256, rows), 0)
    j = k & 127
    block = 2 * ((lax.axis_index("y") + (j >> 4)) & 7) + (((j >> 3) & 1) ^ lax.axis_index("core"))
    source = CAP * block + jnp.where(k < 128, j & 7, 8)
    picked = dot(as_bf(iota((256, rows), 1) == source), hidden[...]).astype(BF)
    row = iota((128, 256), 0) & 7
    last = jnp.zeros((128, 256), F32)
    for r in range(8):
        span = slice(256 * r, 256 * r + 256)
        got = dot(picked, w_in[:, span])
        main = got[:128].astype(BF)
        for i, out in enumerate(outs):
            out[:, span] = main[16 * i : 16 * i + 16]
        last = jnp.where(row == r, got[128:], last)
    last = last.astype(BF)
    for i, out in enumerate(outs):
        out[:, width:] = last[16 * i : 16 * i + 16]


def weight_body(hidden, inputs, routes, out):
    rows, units = hidden.shape
    expert = 2 * lax.axis_index("y") + lax.axis_index("core")
    counts = jnp.sum((routes[...] == expert).astype(F32), axis=1, keepdims=True).astype(jnp.int32)
    n = routes.shape[0]
    g = iota((n, rows), 1)
    first = CAP * iota((n, rows), 0)
    live = (g >= first) & (g < first + counts)
    mask = as_bf(jnp.sum(live.astype(F32), axis=0, keepdims=True) > 0.5)
    j = iota((96, units), 0)
    unit = iota((96, units), 1)
    for k in range(4):
        place = ((j & 7) < 6) & (unit == 6 * (12 * k + (j >> 3)) + (j & 7))
        spread = dot(as_bf(place), hidden[...], 1, 1).astype(BF) * mask
        last = dot(spread, inputs[:, 1536:])
        sub = iota(last.shape, 0) & 7
        for w in range(3):
            span = slice(512 * w, 512 * w + 512)
            tile = dot(spread, inputs[:, span])
            tile = jnp.where(sub == 6, pltpu.roll(last, 6 - w, 0), tile)
            tile = jnp.where(sub == 7, pltpu.roll(last, 4 - w, 0), tile)
            out[96 * k : 96 * k + 96, span] = tile.astype(BF)


def sum_body(scale, parts, out):
    total = parts[0:8, :].astype(F32)
    for z in range(1, parts.shape[0] // 8):
        total = total + parts[8 * z : 8 * z + 8, :].astype(F32)
    total = total / scale
    for u in range(6):
        v, w = u // 3, u % 3
        out[u, :, :1536] = total[u : u + 1, :]
        out[u, :, 1536:] = total[6 + v : 7 + v, 512 * w : 512 * w + 512]


def token_body(routes, residual, far, *rest):
    near = jnp.concatenate([p[...] for p in rest[:-1]], axis=0)
    out = rest[-1]
    ids = routes[...]
    n = ids.shape[1]
    onehot = (iota((16, n), 0) == ids).astype(F32)
    before = as_bf(iota((n, n), 0) < iota((n, n), 1))
    prefix = dot(onehot.astype(BF), before)
    slot = jnp.sum(onehot * prefix, axis=0, keepdims=True).astype(jnp.int32)
    back = (lax.axis_index("y") - (ids >> 1)) & 7
    here = (ids & 1) == lax.axis_index("core")
    k = iota((near.shape[0], n), 0)
    same_near = here & ((k >> 3) == 2 * back)
    c_near = k & 7
    k = iota((far.shape[0], n), 0)
    same_far = jnp.logical_not(here) & ((k >> 3) == back)
    c_far = k & 7
    pick_near = as_bf(same_near & (c_near == slot))
    pick_far = as_bf(same_far & (c_far == slot))
    last_near = near[:, 2048:]
    last_far = far[:, 2048:]
    for r in range(8):
        span = slice(256 * r, 256 * r + 256)
        tail_near = as_bf(same_near & (slot == 8) & (c_near == r))
        tail_far = as_bf(same_far & (slot == 8) & (c_far == r))
        got = dot(pick_near, near[:, span], 0, 0) + dot(pick_far, far[:, span], 0, 0)
        got = got + dot(tail_near, last_near, 0, 0) + dot(tail_far, last_far, 0, 0)
        out[:, span] = (residual[:, span].astype(F32) + got).astype(BF)


def shards(routes, residual_grad, saved_inputs, saved_preact, expert_grad, w_in, w_out):
    S = jax.ShapeDtypeStruct
    slots, width = saved_inputs.shape[1:]
    units = w_in.shape[1]
    groups = Z_DEV * X_DEV
    ids = routes.reshape(1, 128)
    hbm = pl.BlockSpec(memory_space=pl.ANY)
    experts = ("y", "core")
    everyone = lax.all_to_all(
        jnp.broadcast_to(ids[:, None], (16, 1, 128)), experts, split_axis=0, concat_axis=0, tiled=True
    ).reshape(16, 128)
    (hidden,) = call(
        hidden_body,
        [S((slots, units), BF)],
        expert_grad[0], w_out[0], saved_preact[0],
        flops=2 * slots * units * width,
        limit=63,
        in_specs=[hbm] * 3,
        scratch_shapes=[
            pltpu.VMEM((slots, width), BF),
            pltpu.VMEM((units, width), BF),
            pltpu.VMEM((slots, units), BF),
            pltpu.SemaphoreType.DMA((2 * PARTS + 1,)),
        ],
    )
    (part,) = call(
        weight_body, [S((8 * groups, 1536), BF)], hidden, saved_inputs[0], everyone,
        flops=2 * slots * 384 * width,
    )
    hidden, part = lax.optimization_barrier((hidden, part))
    part = lax.all_to_all(part, ("z", "x"), split_axis=0, concat_axis=0, tiled=True)
    pieces = call(
        slot_body, [S((16, width + 256), BF)] * 8, hidden, w_in[0],
        flops=4 * 128 * units * width,
    )
    near = [pieces[0]] + [None] * 7
    for i in (4, 3, 5, 2, 6, 1, 7):
        near[i] = lax.ppermute(pieces[i], "y", [(j, (j + i) % 8) for j in range(8)])
    far = lax.ppermute(jnp.concatenate([p[8:] for p in near], axis=0), "core", [(0, 1), (1, 0)])
    (token_grad,) = call(
        token_body, [S((128, width), BF)], ids, residual_grad, far, *near,
        flops=6 * 128 * 128 * width,
    )
    token_grad, part = lax.optimization_barrier((token_grad, part))
    (grad_in,) = call(
        functools.partial(sum_body, float(groups)), [S((6, 1, width), F32)], part
    )
    return token_grad, jnp.transpose(grad_in, (1, 0, 2))


def solution(mesh):
    fine = Mesh(mesh.devices.reshape(8, 2, Z_DEV, X_DEV), ("y", "core", "z", "x"))
    tokens = P(("y", "core", "z", "x"), None)
    buffers = P(("y", "core"), ("z", "x"), None)
    weights = P(("y", "core"), None, None)
    return jax.shard_map(
        shards,
        mesh=fine,
        in_specs=(tokens, tokens, buffers, buffers, buffers, weights, weights),
        out_specs=(tokens, buffers),
        check_vma=False,
    )
```

```python
import functools
import math
import jax
import jax.numpy as jnp
from jax import lax
from jax.experimental import pallas as pl
from jax.experimental.pallas import tpu as pltpu
from jax.sharding import Mesh, PartitionSpec as P

BF = jnp.bfloat16
F32 = jnp.float32
CAP = 9
X_DEV = 4
Z_DEV = 12
PARTS = 4
MIB = 1024 * 1024


def iota(shape, axis):
    return lax.broadcasted_iota(jnp.int32, shape, axis)


def as_bf(mask):
    return mask.astype(F32).astype(BF)


def dot(a, b, ca=1, cb=0):
    return lax.dot_general(a, b, (((ca,), (cb,)), ((), ())), preferred_element_type=F32)


def call(body, outs, *args, flops=0, limit=32, **more):
    size = sum(math.prod(a.shape) * a.dtype.itemsize for a in (*args, *outs))
    return pl.pallas_call(
        body,
        out_shape=outs,
        compiler_params=pltpu.CompilerParams(vmem_limit_bytes=limit * MIB),
        cost_estimate=pl.CostEstimate(flops=flops, bytes_accessed=size, transcendentals=0),
        **more,
    )(*args)


def hidden_body(grad, w_out, preact, hidden, grad_v, w_out_v, preact_v, sems):
    width = grad.shape[1]
    part = width // PARTS
    loads = []
    for i in range(PARTS):
        span = pl.ds(i * part, part)
        loads.append(pltpu.make_async_copy(grad.at[:, span], grad_v.at[:, span], sems.at[2 * i]))
        loads.append(pltpu.make_async_copy(w_out.at[:, span], w_out_v.at[:, span], sems.at[2 * i + 1]))
    preact_copy = pltpu.make_async_copy(preact, preact_v, sems.at[2 * PARTS])
    for c in loads:
        c.start()
    preact_copy.start()
    product = jnp.zeros(hidden.shape, F32)
    for i in range(PARTS):
        loads[2 * i].wait()
        loads[2 * i + 1].wait()
        span = slice(i * part, i * part + part)
        product = product + dot(grad_v[:, span], w_out_v[:, span], 1, 1)
    preact_copy.wait()
    hidden[...] = jnp.where(preact_v[...].astype(F32) > 0, product, 0.0).astype(BF)


def slot_body(hidden, w_in, slots):
    rows = hidden.shape[0]
    width = w_in.shape[1]
    k = iota((256, rows), 0)
    j = k & 127
    block = 2 * (j >> 4) + (((j >> 3) & 1) ^ lax.axis_index("core"))
    source = CAP * block + jnp.where(k < 128, j & 7, 8)
    picked = dot(as_bf(iota((256, rows), 1) == source), hidden[...]).astype(BF)
    row = iota((128, 256), 0) & 7
    last = jnp.zeros((128, 256), F32)
    for r in range(8):
        span = slice(256 * r, 256 * r + 256)
        got = dot(picked, w_in[:, span])
        slots[:, span] = got[:128].astype(BF)
        last = jnp.where(row == r, got[128:], last)
    slots[:, width:] = last.astype(BF)


def weight_body(hidden, inputs, routes, *outs):
    rows, units = hidden.shape
    expert = 2 * lax.axis_index("y") + lax.axis_index("core")
    counts = jnp.sum((routes[...] == expert).astype(F32), axis=1, keepdims=True).astype(jnp.int32)
    j = iota((96, units), 0)
    unit = iota((96, units), 1)
    n = routes.shape[0]
    g = iota((n, rows), 1)
    first = CAP * iota((n, rows), 0)
    live = (g >= first) & (g < first + counts)
    mask = as_bf(jnp.sum(live.astype(F32), axis=0, keepdims=True) > 0.5)
    me = lax.axis_index("x")
    for k, out in enumerate(outs):
        owner = X_DEV * (j >> 3) + ((me + k) & 3)
        place = ((j & 7) < 6) & (unit == 6 * owner + (j & 7))
        spread = dot(as_bf(place), hidden[...], 1, 1).astype(BF) * mask
        last = dot(spread, inputs[:, 1536:])
        sub = iota(last.shape, 0) & 7
        for w in range(3):
            span = slice(512 * w, 512 * w + 512)
            tile = dot(spread, inputs[:, span])
            tile = jnp.where(sub == 6, pltpu.roll(last, 6 - w, 0), tile)
            tile = jnp.where(sub == 7, pltpu.roll(last, 4 - w, 0), tile)
            out[:, span] = tile.astype(BF)


def add_body(own, one, two, three, out):
    total = (own[...].astype(F32) + one[...].astype(F32)) + (two[...].astype(F32) + three[...].astype(F32))
    out[...] = total.astype(BF)


def sum_body(scale, parts, out):
    total = parts[0:8, :].astype(F32)
    for z in range(1, parts.shape[0] // 8):
        total = total + parts[8 * z : 8 * z + 8, :].astype(F32)
    total = total / scale
    for u in range(6):
        v, w = u // 3, u % 3
        out[u, :, :1536] = total[u : u + 1, :]
        out[u, :, 1536:] = total[6 + v : 7 + v, 512 * w : 512 * w + 512]


def token_body(routes, residual, near, far, out):
    ids = routes[...]
    n = ids.shape[1]
    onehot = (iota((16, n), 0) == ids).astype(F32)
    before = as_bf(iota((n, n), 0) < iota((n, n), 1))
    prefix = dot(onehot.astype(BF), before)
    slot = jnp.sum(onehot * prefix, axis=0, keepdims=True).astype(jnp.int32)
    here = (ids & 1) == lax.axis_index("core")
    k = iota((near.shape[0], n), 0)
    same_near = here & ((k >> 3) == 2 * (ids >> 1))
    c_near = k & 7
    k = iota((far.shape[0], n), 0)
    same_far = jnp.logical_not(here) & ((k >> 3) == (ids >> 1))
    c_far = k & 7
    pick_near = as_bf(same_near & (c_near == slot))
    pick_far = as_bf(same_far & (c_far == slot))
    last_near = near[:, 2048:]
    last_far = far[:, 2048:]
    for r in range(8):
        span = slice(256 * r, 256 * r + 256)
        tail_near = as_bf(same_near & (slot == 8) & (c_near == r))
        tail_far = as_bf(same_far & (slot == 8) & (c_far == r))
        got = dot(pick_near, near[:, span], 0, 0) + dot(pick_far, far[:, span], 0, 0)
        got = got + dot(tail_near, last_near, 0, 0) + dot(tail_far, last_far, 0, 0)
        out[:, span] = (residual[:, span].astype(F32) + got).astype(BF)


def shards(routes, residual_grad, saved_inputs, saved_preact, expert_grad, w_in, w_out):
    S = jax.ShapeDtypeStruct
    slots, width = saved_inputs.shape[1:]
    units = w_in.shape[1]
    groups = lax.axis_size("z") * lax.axis_size("x")
    ids = routes.reshape(1, 128)
    hbm = pl.BlockSpec(memory_space=pl.ANY)
    experts = ("y", "core")
    everyone = lax.all_to_all(
        jnp.broadcast_to(ids[:, None], (16, 1, 128)), experts, split_axis=0, concat_axis=0, tiled=True
    ).reshape(16, 128)
    (hidden,) = call(
        hidden_body,
        [pltpu.VMEM((slots, units), BF)],
        *[pltpu.with_memory_space_constraint(a[0], pltpu.HBM) for a in (expert_grad, w_out, saved_preact)],
        flops=2 * slots * units * width,
        in_specs=[hbm] * 3,
        scratch_shapes=[
            pltpu.VMEM((slots, width), BF),
            pltpu.VMEM((units, width), BF),
            pltpu.VMEM((slots, units), BF),
            pltpu.SemaphoreType.DMA((2 * PARTS + 1,)),
        ],
    )
    (slot_grad,) = call(
        slot_body, [S((128, width + 256), BF)], hidden, w_in[0], flops=4 * 128 * units * width
    )
    sends = call(
        weight_body, [S((8 * Z_DEV, 1536), BF)] * X_DEV, hidden, saved_inputs[0], everyone,
        flops=2 * slots * 384 * width,
    )
    *sends, slot_grad = lax.optimization_barrier((*sends, slot_grad))
    near = lax.all_to_all(slot_grad, "y", split_axis=0, concat_axis=0, tiled=True)
    far = near.reshape(8, 2, 8, width + 256)[:, 1].reshape(64, width + 256)
    far = lax.ppermute(far, "core", [(0, 1), (1, 0)])
    got = [sends[0]]
    for i in (2, 1, 3):
        got.append(lax.ppermute(sends[i], "x", [(j, (j + i) % X_DEV) for j in range(X_DEV)]))
    (part,) = call(add_body, [S((8 * Z_DEV, 1536), BF)], *got)
    part = lax.all_to_all(part, "z", split_axis=0, concat_axis=0, tiled=True)
    (token_grad,) = call(
        token_body, [S((128, width), BF)], ids, residual_grad, near, far,
        flops=6 * 128 * 128 * width,
    )
    token_grad, part = lax.optimization_barrier((token_grad, part))
    (grad_in,) = call(
        functools.partial(sum_body, float(groups)), [S((6, 1, width), F32)], part
    )
    return token_grad, jnp.transpose(grad_in, (1, 0, 2))


def solution(mesh):
    fine = Mesh(mesh.devices.reshape(8, 2, Z_DEV, X_DEV), ("y", "core", "z", "x"))
    tokens = P(("y", "core", "z", "x"), None)
    buffers = P(("y", "core"), ("z", "x"), None)
    weights = P(("y", "core"), None, None)
    return jax.shard_map(
        shards,
        mesh=fine,
        in_specs=(tokens, tokens, buffers, buffers, buffers, weights, weights),
        out_specs=(tokens, buffers),
        check_vma=False,
    )
```

```python
import functools
import math
import jax
import jax.numpy as jnp
from jax import lax
from jax.experimental import pallas as pl
from jax.experimental.pallas import tpu as pltpu
from jax.sharding import Mesh, PartitionSpec as P

BF = jnp.bfloat16
F32 = jnp.float32
CAP = 9
X_DEV = 4
Z_DEV = 12
PARTS = 4
MIB = 1024 * 1024


def iota(shape, axis):
    return lax.broadcasted_iota(jnp.int32, shape, axis)


def as_bf(mask):
    return mask.astype(F32).astype(BF)


def dot(a, b, ca=1, cb=0):
    return lax.dot_general(a, b, (((ca,), (cb,)), ((), ())), preferred_element_type=F32)


def call(body, outs, *args, flops=0, limit=32, **more):
    size = sum(math.prod(a.shape) * a.dtype.itemsize for a in (*args, *outs))
    return pl.pallas_call(
        body,
        out_shape=outs,
        compiler_params=pltpu.CompilerParams(vmem_limit_bytes=limit * MIB),
        cost_estimate=pl.CostEstimate(flops=flops, bytes_accessed=size, transcendentals=0),
        **more,
    )(*args)


def hidden_body(grad, w_out, preact, hidden, grad_v, w_out_v, preact_v, sems):
    width = grad.shape[1]
    part = width // PARTS
    loads = []
    for i in range(PARTS):
        span = pl.ds(i * part, part)
        loads.append(pltpu.make_async_copy(grad.at[:, span], grad_v.at[:, span], sems.at[2 * i]))
        loads.append(pltpu.make_async_copy(w_out.at[:, span], w_out_v.at[:, span], sems.at[2 * i + 1]))
    preact_copy = pltpu.make_async_copy(preact, preact_v, sems.at[2 * PARTS])
    for c in loads:
        c.start()
    preact_copy.start()
    product = jnp.zeros(hidden.shape, F32)
    for i in range(PARTS):
        loads[2 * i].wait()
        loads[2 * i + 1].wait()
        span = slice(i * part, i * part + part)
        product = product + dot(grad_v[:, span], w_out_v[:, span], 1, 1)
    preact_copy.wait()
    hidden[...] = jnp.where(preact_v[...].astype(F32) > 0, product, 0.0).astype(BF)


def slot_body(hidden, w_in, slots):
    rows = hidden.shape[0]
    width = w_in.shape[1]
    k = iota((256, rows), 0)
    j = k & 127
    block = 2 * (j >> 4) + (((j >> 3) & 1) ^ lax.axis_index("core"))
    source = CAP * block + jnp.where(k < 128, j & 7, 8)
    picked = dot(as_bf(iota((256, rows), 1) == source), hidden[...]).astype(BF)
    row = iota((128, 256), 0) & 7
    last = jnp.zeros((128, 256), F32)
    for r in range(8):
        span = slice(256 * r, 256 * r + 256)
        got = dot(picked, w_in[:, span])
        slots[:, span] = got[:128].astype(BF)
        last = jnp.where(row == r, got[128:], last)
    slots[:, width:] = last.astype(BF)


def weight_body(steps, hidden, inputs, routes, *outs):
    rows, units = hidden.shape
    expert = 2 * lax.axis_index("y") + lax.axis_index("core")
    counts = jnp.sum((routes[...] == expert).astype(F32), axis=1, keepdims=True).astype(jnp.int32)
    j = iota((96, units), 0)
    unit = iota((96, units), 1)
    n = routes.shape[0]
    g = iota((n, rows), 1)
    first = CAP * iota((n, rows), 0)
    live = (g >= first) & (g < first + counts)
    mask = as_bf(jnp.sum(live.astype(F32), axis=0, keepdims=True) > 0.5)
    for step, out in zip(steps, outs):
        owner = X_DEV * (j >> 3) + step()
        place = ((j & 7) < 6) & (unit == 6 * owner + (j & 7))
        spread = dot(as_bf(place), hidden[...], 1, 1).astype(BF) * mask
        last = dot(spread, inputs[:, 1536:])
        sub = iota(last.shape, 0) & 7
        for w in range(3):
            span = slice(512 * w, 512 * w + 512)
            tile = dot(spread, inputs[:, span])
            tile = jnp.where(sub == 6, pltpu.roll(last, 6 - w, 0), tile)
            tile = jnp.where(sub == 7, pltpu.roll(last, 4 - w, 0), tile)
            out[:, span] = tile.astype(BF)


def pair_body(hidden, inputs, routes, out):
    n = out.shape[0] // 2
    halves = [out.at[pl.ds(h * n, n), :] for h in range(2)]
    steps = [functools.partial(lambda h: 2 * h + lax.axis_index("xl"), h) for h in range(2)]
    weight_body(steps, hidden, inputs, routes, *halves)


def side_body(hidden, inputs, routes, *outs):
    me = 2 * lax.axis_index("xh") + lax.axis_index("xl")
    weight_body([lambda: (me + 1) & 3, lambda: (me + 3) & 3], hidden, inputs, routes, *outs)


def add_body(pair, one, three, out):
    total = pair[...].astype(F32) + (one[...].astype(F32) + three[...].astype(F32))
    out[...] = total.astype(BF)


def sum_body(scale, parts, out):
    total = parts[0:8, :].astype(F32)
    for z in range(1, parts.shape[0] // 8):
        total = total + parts[8 * z : 8 * z + 8, :].astype(F32)
    total = total / scale
    for u in range(6):
        v, w = u // 3, u % 3
        out[u, :, :1536] = total[u : u + 1, :]
        out[u, :, 1536:] = total[6 + v : 7 + v, 512 * w : 512 * w + 512]


def token_body(routes, residual, near, far, out):
    ids = routes[...]
    n = ids.shape[1]
    onehot = (iota((16, n), 0) == ids).astype(F32)
    before = as_bf(iota((n, n), 0) < iota((n, n), 1))
    prefix = dot(onehot.astype(BF), before)
    slot = jnp.sum(onehot * prefix, axis=0, keepdims=True).astype(jnp.int32)
    here = (ids & 1) == lax.axis_index("core")
    k = iota((near.shape[0], n), 0)
    same_near = here & ((k >> 3) == 2 * (ids >> 1))
    c_near = k & 7
    k = iota((far.shape[0], n), 0)
    same_far = jnp.logical_not(here) & ((k >> 3) == (ids >> 1))
    c_far = k & 7
    pick_near = as_bf(same_near & (c_near == slot))
    pick_far = as_bf(same_far & (c_far == slot))
    last_near = near[:, 2048:]
    last_far = far[:, 2048:]
    for r in range(8):
        span = slice(256 * r, 256 * r + 256)
        tail_near = as_bf(same_near & (slot == 8) & (c_near == r))
        tail_far = as_bf(same_far & (slot == 8) & (c_far == r))
        got = dot(pick_near, near[:, span], 0, 0) + dot(pick_far, far[:, span], 0, 0)
        got = got + dot(tail_near, last_near, 0, 0) + dot(tail_far, last_far, 0, 0)
        out[:, span] = (residual[:, span].astype(F32) + got).astype(BF)


def shards(routes, residual_grad, saved_inputs, saved_preact, expert_grad, w_in, w_out):
    S = jax.ShapeDtypeStruct
    slots, width = saved_inputs.shape[1:]
    units = w_in.shape[1]
    groups = Z_DEV * X_DEV
    ids = routes.reshape(1, 128)
    hbm = pl.BlockSpec(memory_space=pl.ANY)
    experts = ("y", "core")
    everyone = lax.all_to_all(
        jnp.broadcast_to(ids[:, None], (16, 1, 128)), experts, split_axis=0, concat_axis=0, tiled=True
    ).reshape(16, 128)
    (hidden,) = call(
        hidden_body,
        [pltpu.VMEM((slots, units), BF)],
        *[pltpu.with_memory_space_constraint(a[0], pltpu.HBM) for a in (expert_grad, w_out, saved_preact)],
        flops=2 * slots * units * width,
        in_specs=[hbm] * 3,
        scratch_shapes=[
            pltpu.VMEM((slots, width), BF),
            pltpu.VMEM((units, width), BF),
            pltpu.VMEM((slots, units), BF),
            pltpu.SemaphoreType.DMA((2 * PARTS + 1,)),
        ],
    )
    (slot_grad,) = call(
        slot_body, [S((128, width + 256), BF)], hidden, w_in[0], flops=4 * 128 * units * width
    )
    def products(body, outs, hidden):
        return call(body, outs, hidden, saved_inputs[0], everyone, flops=4 * slots * 96 * width)

    def shift(send, i):
        return lax.ppermute(send, ("xh", "xl"), [(j, (j + i) % X_DEV) for j in range(X_DEV)])

    rows = 8 * Z_DEV
    (pair,) = products(pair_body, [S((2 * rows, 1536), BF)], hidden)
    hidden, pair = lax.optimization_barrier((hidden, pair))
    pair = lax.psum_scatter(pair, "xh", scatter_dimension=0, tiled=True)
    right, left = products(side_body, [S((rows, 1536), BF)] * 2, hidden)
    right, left, slot_grad = lax.optimization_barrier((right, left, slot_grad))
    near = lax.all_to_all(slot_grad, "y", split_axis=0, concat_axis=0, tiled=True)
    got = [pair, shift(right, 1), shift(left, 3)]
    far = near.reshape(8, 2, 8, width + 256)[:, 1].reshape(64, width + 256)
    far = lax.ppermute(far, "core", [(0, 1), (1, 0)])
    (part,) = call(add_body, [S((8 * Z_DEV, 1536), BF)], *got)
    part = lax.all_to_all(part, "z", split_axis=0, concat_axis=0, tiled=True)
    (token_grad,) = call(
        token_body, [S((128, width), BF)], ids, residual_grad, near, far,
        flops=6 * 128 * 128 * width,
    )
    token_grad, part = lax.optimization_barrier((token_grad, part))
    (grad_in,) = call(
        functools.partial(sum_body, float(groups)), [S((6, 1, width), F32)], part
    )
    return token_grad, jnp.transpose(grad_in, (1, 0, 2))


def solution(mesh):
    fine = Mesh(mesh.devices.reshape(8, 2, Z_DEV, 2, 2), ("y", "core", "z", "xh", "xl"))
    tokens = P(("y", "core", "z", "xh", "xl"), None)
    buffers = P(("y", "core"), ("z", "xh", "xl"), None)
    weights = P(("y", "core"), None, None)
    return jax.shard_map(
        shards,
        mesh=fine,
        in_specs=(tokens, tokens, buffers, buffers, buffers, weights, weights),
        out_specs=(tokens, buffers),
        check_vma=False,
    )
```

```python
import functools
import math
import jax
import jax.numpy as jnp
from jax import lax
from jax.experimental import pallas as pl
from jax.experimental.pallas import tpu as pltpu
from jax.sharding import Mesh, PartitionSpec as P

BF = jnp.bfloat16
F32 = jnp.float32
CAP = 9
X_DEV = 4
Z_DEV = 12
AHEAD = 10_000_000_000
MIB = 1024 * 1024


def iota(shape, axis):
    return lax.broadcasted_iota(jnp.int32, shape, axis)


def as_bf(mask):
    return mask.astype(F32).astype(BF)


def dot(a, b, ca=1, cb=0):
    return lax.dot_general(a, b, (((ca,), (cb,)), ((), ())), preferred_element_type=F32)


def call(body, outs, *args, flops=0, limit=32, **more):
    size = sum(math.prod(a.shape) * a.dtype.itemsize for a in (*args, *outs))
    return pl.pallas_call(
        body,
        out_shape=outs,
        compiler_params=pltpu.CompilerParams(vmem_limit_bytes=limit * MIB),
        cost_estimate=pl.CostEstimate(flops=flops, bytes_accessed=size, transcendentals=0),
        **more,
    )(*args)


def spread_body(routes, out):
    out[...] = jnp.broadcast_to(routes[...], out.shape)


def hidden_body(grad, w_out, preact, hidden):
    product = dot(grad[...], w_out[...], 1, 1)
    hidden[...] = jnp.where(preact[...].astype(F32) > 0, product, 0.0).astype(BF)


def slot_body(hidden, w_in, slots):
    rows = hidden.shape[0]
    width = w_in.shape[1]
    k = iota((256, rows), 0)
    j = k & 127
    block = 2 * (j >> 4) + (((j >> 3) & 1) ^ lax.axis_index("core"))
    source = CAP * block + jnp.where(k < 128, j & 7, 8)
    picked = dot(as_bf(iota((256, rows), 1) == source), hidden[...]).astype(BF)
    row = iota((128, 256), 0) & 7
    last = jnp.zeros((128, 256), F32)
    for r in range(8):
        span = slice(256 * r, 256 * r + 256)
        got = dot(picked, w_in[:, span])
        slots[:, span] = got[:128].astype(BF)
        last = jnp.where(row == r, got[128:], last)
    slots[:, width:] = last.astype(BF)


def weight_body(hidden, inputs, routes, *outs):
    rows, units = hidden.shape
    expert = 2 * lax.axis_index("y") + lax.axis_index("core")
    counts = jnp.sum((routes[...] == expert).astype(F32), axis=1, keepdims=True).astype(jnp.int32)
    j = iota((96, units), 0)
    unit = iota((96, units), 1)
    n = routes.shape[0]
    g = iota((n, rows), 1)
    first = CAP * iota((n, rows), 0)
    live = (g >= first) & (g < first + counts)
    mask = as_bf(jnp.sum(live.astype(F32), axis=0, keepdims=True) > 0.5)
    me = lax.axis_index("x")
    for k, out in enumerate(outs):
        owner = X_DEV * (j >> 3) + ((me + k) & 3)
        place = ((j & 7) < 6) & (unit == 6 * owner + (j & 7))
        spread = dot(as_bf(place), hidden[...], 1, 1).astype(BF) * mask
        last = dot(spread, inputs[:, 1536:])
        sub = iota(last.shape, 0) & 7
        for w in range(3):
            span = slice(512 * w, 512 * w + 512)
            tile = dot(spread, inputs[:, span])
            tile = jnp.where(sub == 6, pltpu.roll(last, 6 - w, 0), tile)
            tile = jnp.where(sub == 7, pltpu.roll(last, 4 - w, 0), tile)
            out[:, span] = tile.astype(BF)


def first_add_body(own, opposite, out):
    out[...] = own[...].astype(F32) + opposite[...].astype(F32)


def add_body(pair, one, three, out):
    total = pair[...] + (one[...].astype(F32) + three[...].astype(F32))
    out[...] = total.astype(BF)


def sum_body(scale, parts, out):
    total = parts[0:8, :].astype(F32)
    for z in range(1, parts.shape[0] // 8):
        total = total + parts[8 * z : 8 * z + 8, :].astype(F32)
    total = total / scale
    for u in range(6):
        v, w = u // 3, u % 3
        out[u, :, :1536] = total[u : u + 1, :]
        out[u, :, 1536:] = total[6 + v : 7 + v, 512 * w : 512 * w + 512]


def token_body(routes, residual, near, far, out):
    ids = routes[...]
    n = ids.shape[1]
    onehot = (iota((16, n), 0) == ids).astype(F32)
    before = as_bf(iota((n, n), 0) < iota((n, n), 1))
    prefix = dot(onehot.astype(BF), before)
    slot = jnp.sum(onehot * prefix, axis=0, keepdims=True).astype(jnp.int32)
    here = (ids & 1) == lax.axis_index("core")
    k = iota((near.shape[0], n), 0)
    same_near = here & ((k >> 3) == 2 * (ids >> 1))
    c_near = k & 7
    k = iota((far.shape[0], n), 0)
    same_far = jnp.logical_not(here) & ((k >> 3) == (ids >> 1))
    c_far = k & 7
    pick_near = as_bf(same_near & (c_near == slot))
    pick_far = as_bf(same_far & (c_far == slot))
    last_near = near[:, 2048:]
    last_far = far[:, 2048:]
    for r in range(8):
        span = slice(256 * r, 256 * r + 256)
        tail_near = as_bf(same_near & (slot == 8) & (c_near == r))
        tail_far = as_bf(same_far & (slot == 8) & (c_far == r))
        got = dot(pick_near, near[:, span], 0, 0) + dot(pick_far, far[:, span], 0, 0)
        got = got + dot(tail_near, last_near, 0, 0) + dot(tail_far, last_far, 0, 0)
        out[:, span] = (residual[:, span].astype(F32) + got).astype(BF)


def shards(routes, residual_grad, saved_inputs, saved_preact, expert_grad, w_in, w_out):
    S = jax.ShapeDtypeStruct
    slots, width = saved_inputs.shape[1:]
    units = w_in.shape[1]
    groups = lax.axis_size("z") * lax.axis_size("x")
    ids = routes.reshape(1, 128)
    experts = ("y", "core")
    (everyone,) = call(spread_body, [S((16, 128), jnp.int32)], ids, flops=AHEAD)
    everyone = lax.all_to_all(
        everyone.reshape(16, 1, 128), experts, split_axis=0, concat_axis=0, tiled=True
    ).reshape(16, 128)
    (hidden,) = call(
        hidden_body,
        [pltpu.VMEM((slots, units), BF)],
        *[pltpu.with_memory_space_constraint(a[0], pltpu.VMEM) for a in (expert_grad, w_out, saved_preact)],
        flops=2 * slots * units * width,
    )
    (slot_grad,) = call(
        slot_body, [S((128, width + 256), BF)], hidden, w_in[0], flops=4 * 128 * units * width
    )
    sends = call(
        weight_body, [S((8 * Z_DEV, 1536), BF)] * X_DEV, hidden, saved_inputs[0], everyone,
        flops=2 * slots * 384 * width,
    )
    *sends, slot_grad = lax.optimization_barrier((*sends, slot_grad))
    near = lax.all_to_all(slot_grad, "y", split_axis=0, concat_axis=0, tiled=True)
    far = near.reshape(8, 2, 8, width + 256)[:, 1].reshape(64, width + 256)
    far = lax.ppermute(far, "core", [(0, 1), (1, 0)])
    def shift(i):
        return lax.ppermute(sends[i], "x", [(j, (j + i) % X_DEV) for j in range(X_DEV)])

    rows = 8 * Z_DEV
    (pair,) = call(first_add_body, [S((rows, 1536), F32)], sends[0], shift(2), flops=AHEAD)
    (part,) = call(add_body, [S((rows, 1536), BF)], pair, shift(1), shift(3))
    part = lax.all_to_all(part, "z", split_axis=0, concat_axis=0, tiled=True)
    (token_grad,) = call(
        token_body, [S((128, width), BF)], ids, residual_grad, near, far,
        flops=6 * 128 * 128 * width,
    )
    token_grad, part = lax.optimization_barrier((token_grad, part))
    (grad_in,) = call(
        functools.partial(sum_body, float(groups)), [S((6, 1, width), F32)], part
    )
    return token_grad, jnp.transpose(grad_in, (1, 0, 2))


def solution(mesh):
    fine = Mesh(mesh.devices.reshape(8, 2, Z_DEV, X_DEV), ("y", "core", "z", "x"))
    tokens = P(("y", "core", "z", "x"), None)
    buffers = P(("y", "core"), ("z", "x"), None)
    weights = P(("y", "core"), None, None)
    return jax.shard_map(
        shards,
        mesh=fine,
        in_specs=(tokens, tokens, buffers, buffers, buffers, weights, weights),
        out_specs=(tokens, buffers),
        check_vma=False,
    )
```

```python
import functools
import math
import jax
import jax.numpy as jnp
from jax import lax
from jax.experimental import pallas as pl
from jax.experimental.pallas import tpu as pltpu
from jax.sharding import Mesh, PartitionSpec as P

BF = jnp.bfloat16
F32 = jnp.float32
CAP = 9
X_DEV = 4
Z_DEV = 12
AHEAD = 10_000_000_000
MIB = 1024 * 1024


def iota(shape, axis):
    return lax.broadcasted_iota(jnp.int32, shape, axis)


def as_bf(mask):
    return mask.astype(F32).astype(BF)


def dot(a, b, ca=1, cb=0):
    return lax.dot_general(a, b, (((ca,), (cb,)), ((), ())), preferred_element_type=F32)


def call(body, outs, *args, flops=0, limit=32, **more):
    size = sum(math.prod(a.shape) * a.dtype.itemsize for a in (*args, *outs))
    return pl.pallas_call(
        body,
        out_shape=outs,
        compiler_params=pltpu.CompilerParams(vmem_limit_bytes=limit * MIB),
        cost_estimate=pl.CostEstimate(flops=flops, bytes_accessed=size, transcendentals=0),
        **more,
    )(*args)


def spread_body(routes, out):
    out[...] = jnp.broadcast_to(routes[...], out.shape)


def hidden_body(grad, w_out, preact, hidden):
    product = dot(grad[...], w_out[...], 1, 1)
    hidden[...] = jnp.where(preact[...].astype(F32) > 0, product, 0.0).astype(BF)


def slot_body(hidden, w_in, slots):
    rows = hidden.shape[0]
    width = w_in.shape[1]
    k = iota((256, rows), 0)
    j = k & 127
    block = 2 * (j >> 4) + (((j >> 3) & 1) ^ lax.axis_index("core"))
    source = CAP * block + jnp.where(k < 128, j & 7, 8)
    picked = dot(as_bf(iota((256, rows), 1) == source), hidden[...]).astype(BF)
    row = iota((128, 256), 0) & 7
    last = jnp.zeros((128, 256), F32)
    for r in range(8):
        span = slice(256 * r, 256 * r + 256)
        got = dot(picked, w_in[:, span])
        slots[:, span] = got[:128].astype(BF)
        last = jnp.where(row == r, got[128:], last)
    slots[:, width:] = last.astype(BF)


def weight_body(hidden, inputs, routes, *outs):
    rows, units = hidden.shape
    expert = 2 * lax.axis_index("y") + lax.axis_index("core")
    counts = jnp.sum((routes[...] == expert).astype(F32), axis=1, keepdims=True).astype(jnp.int32)
    j = iota((96, units), 0)
    unit = iota((96, units), 1)
    n = routes.shape[0]
    g = iota((n, rows), 1)
    first = CAP * iota((n, rows), 0)
    live = (g >= first) & (g < first + counts)
    mask = as_bf(jnp.sum(live.astype(F32), axis=0, keepdims=True) > 0.5)
    me = lax.axis_index("x")
    for k, out in enumerate(outs):
        owner = X_DEV * (j >> 3) + ((me + k) & 3)
        place = ((j & 7) < 6) & (unit == 6 * owner + (j & 7))
        spread = dot(as_bf(place), hidden[...], 1, 1).astype(BF) * mask
        last = dot(spread, inputs[:, 1536:])
        sub = iota(last.shape, 0) & 7
        for w in range(3):
            span = slice(512 * w, 512 * w + 512)
            tile = dot(spread, inputs[:, span])
            tile = jnp.where(sub == 6, pltpu.roll(last, 6 - w, 0), tile)
            tile = jnp.where(sub == 7, pltpu.roll(last, 4 - w, 0), tile)
            out[:, span] = tile.astype(BF)


def add_body(own, one, two, three, out):
    total = (own[...].astype(F32) + one[...].astype(F32)) + (two[...].astype(F32) + three[...].astype(F32))
    out[...] = total.astype(BF)


def sum_body(scale, parts, out):
    total = parts[0:8, :].astype(F32)
    for z in range(1, parts.shape[0] // 8):
        total = total + parts[8 * z : 8 * z + 8, :].astype(F32)
    total = total / scale
    for u in range(6):
        v, w = u // 3, u % 3
        out[u, :, :1536] = total[u : u + 1, :]
        out[u, :, 1536:] = total[6 + v : 7 + v, 512 * w : 512 * w + 512]


def token_body(routes, residual, near, far, out):
    ids = routes[...]
    n = ids.shape[1]
    onehot = (iota((16, n), 0) == ids).astype(F32)
    before = as_bf(iota((n, n), 0) < iota((n, n), 1))
    prefix = dot(onehot.astype(BF), before)
    slot = jnp.sum(onehot * prefix, axis=0, keepdims=True).astype(jnp.int32)
    here = (ids & 1) == lax.axis_index("core")
    k = iota((near.shape[0], n), 0)
    same_near = here & ((k >> 3) == 2 * (ids >> 1))
    c_near = k & 7
    k = iota((far.shape[0], n), 0)
    same_far = jnp.logical_not(here) & ((k >> 3) == (ids >> 1))
    c_far = k & 7
    pick_near = as_bf(same_near & (c_near == slot))
    pick_far = as_bf(same_far & (c_far == slot))
    last_near = near[:, 2048:]
    last_far = far[:, 2048:]
    for r in range(8):
        span = slice(256 * r, 256 * r + 256)
        tail_near = as_bf(same_near & (slot == 8) & (c_near == r))
        tail_far = as_bf(same_far & (slot == 8) & (c_far == r))
        got = dot(pick_near, near[:, span], 0, 0) + dot(pick_far, far[:, span], 0, 0)
        got = got + dot(tail_near, last_near, 0, 0) + dot(tail_far, last_far, 0, 0)
        out[:, span] = (residual[:, span].astype(F32) + got).astype(BF)


def shards(routes, residual_grad, saved_inputs, saved_preact, expert_grad, w_in, w_out):
    S = jax.ShapeDtypeStruct
    slots, width = saved_inputs.shape[1:]
    units = w_in.shape[1]
    groups = lax.axis_size("z") * lax.axis_size("x")
    ids = routes.reshape(1, 128)
    experts = ("y", "core")
    (everyone,) = call(spread_body, [S((16, 128), jnp.int32)], ids, flops=AHEAD)
    everyone = lax.all_to_all(
        everyone.reshape(16, 1, 128), experts, split_axis=0, concat_axis=0, tiled=True
    ).reshape(16, 128)
    (hidden,) = call(
        hidden_body,
        [pltpu.VMEM((slots, units), BF)],
        *[pltpu.with_memory_space_constraint(a[0], pltpu.VMEM) for a in (expert_grad, w_out, saved_preact)],
        flops=2 * slots * units * width,
    )
    (slot_grad,) = call(
        slot_body, [S((128, width + 256), BF)], hidden, w_in[0], flops=4 * 128 * units * width
    )
    sends = call(
        weight_body, [S((8 * Z_DEV, 1536), BF)] * X_DEV, hidden, saved_inputs[0], everyone,
        flops=2 * slots * 384 * width,
    )
    near = lax.all_to_all(slot_grad, "y", split_axis=0, concat_axis=0, tiled=True)
    far = near.reshape(8, 2, 8, width + 256)[:, 1].reshape(64, width + 256)
    far = lax.ppermute(far, "core", [(0, 1), (1, 0)])
    def shift(i):
        return lax.ppermute(sends[i], "x", [(j, (j + i) % X_DEV) for j in range(X_DEV)])

    (part,) = call(add_body, [S((8 * Z_DEV, 1536), BF)], sends[0], shift(2), shift(1), shift(3))
    part = lax.all_to_all(part, "z", split_axis=0, concat_axis=0, tiled=True)
    (token_grad,) = call(
        token_body, [S((128, width), BF)], ids, residual_grad, near, far,
        flops=6 * 128 * 128 * width,
    )
    token_grad, part = lax.optimization_barrier((token_grad, part))
    (grad_in,) = call(
        functools.partial(sum_body, float(groups)), [S((6, 1, width), F32)], part
    )
    return token_grad, jnp.transpose(grad_in, (1, 0, 2))


def solution(mesh):
    fine = Mesh(mesh.devices.reshape(8, 2, Z_DEV, X_DEV), ("y", "core", "z", "x"))
    tokens = P(("y", "core", "z", "x"), None)
    buffers = P(("y", "core"), ("z", "x"), None)
    weights = P(("y", "core"), None, None)
    return jax.shard_map(
        shards,
        mesh=fine,
        in_specs=(tokens, tokens, buffers, buffers, buffers, weights, weights),
        out_specs=(tokens, buffers),
        check_vma=False,
    )
```

```python
import functools
import math
import jax
import jax.numpy as jnp
from jax import lax
from jax.experimental import pallas as pl
from jax.experimental.pallas import tpu as pltpu
from jax.sharding import Mesh, PartitionSpec as P

BF = jnp.bfloat16
F32 = jnp.float32
CAP = 9
X_DEV = 4
Z_DEV = 12
AHEAD = 10_000_000_000
MIB = 1024 * 1024


def iota(shape, axis):
    return lax.broadcasted_iota(jnp.int32, shape, axis)


def as_bf(mask):
    return mask.astype(F32).astype(BF)


def dot(a, b, ca=1, cb=0):
    return lax.dot_general(a, b, (((ca,), (cb,)), ((), ())), preferred_element_type=F32)


def call(body, outs, *args, flops=0, limit=32, **more):
    size = sum(math.prod(a.shape) * a.dtype.itemsize for a in (*args, *outs))
    return pl.pallas_call(
        body,
        out_shape=outs,
        compiler_params=pltpu.CompilerParams(vmem_limit_bytes=limit * MIB),
        cost_estimate=pl.CostEstimate(flops=flops, bytes_accessed=size, transcendentals=0),
        **more,
    )(*args)


def spread_body(routes, out):
    out[...] = jnp.broadcast_to(routes[...], out.shape)


def hidden_body(grad, w_out, preact, hidden):
    product = dot(grad[...], w_out[...], 1, 1)
    hidden[...] = jnp.where(preact[...].astype(F32) > 0, product, 0.0).astype(BF)


def slot_body(hidden, w_in, slots, spread):
    rows = hidden.shape[0]
    width = w_in.shape[1]
    k = iota((256, rows), 0)
    j = k & 127
    block = 2 * (j >> 4) + (((j >> 3) & 1) ^ lax.axis_index("core"))
    source = CAP * block + jnp.where(k < 128, j & 7, 8)
    picked = dot(as_bf(iota((256, rows), 1) == source), hidden[...]).astype(BF)
    row = iota((128, 256), 0) & 7
    last = jnp.zeros((128, 256), F32)
    for r in range(8):
        span = slice(256 * r, 256 * r + 256)
        got = dot(picked, w_in[:, span])
        slots[:, span] = got[:128].astype(BF)
        last = jnp.where(row == r, got[128:], last)
    slots[:, width:] = last.astype(BF)
    me = lax.axis_index("x")
    units = hidden.shape[1]
    m = spread.shape[0] // X_DEV
    j = iota((m, units), 0)
    unit = iota((m, units), 1)
    for k in range(X_DEV):
        owner = X_DEV * (j >> 3) + ((me + k) & 3)
        place = ((j & 7) < 6) & (unit == 6 * owner + (j & 7))
        spread[m * k : m * k + m, :] = dot(as_bf(place), hidden[...], 1, 1).astype(BF)


def weight_body(spread, inputs, routes, *outs):
    rows = spread.shape[1]
    expert = 2 * lax.axis_index("y") + lax.axis_index("core")
    counts = jnp.sum((routes[...] == expert).astype(F32), axis=1, keepdims=True).astype(jnp.int32)
    n = routes.shape[0]
    g = iota((n, rows), 1)
    first = CAP * iota((n, rows), 0)
    live = (g >= first) & (g < first + counts)
    mask = as_bf(jnp.sum(live.astype(F32), axis=0, keepdims=True) > 0.5)
    gated = spread[...] * mask
    last = dot(gated, inputs[:, 1536:])
    sub = iota(last.shape, 0) & 7
    m = outs[0].shape[0]
    for w in range(3):
        span = slice(512 * w, 512 * w + 512)
        tile = dot(gated, inputs[:, span])
        tile = jnp.where(sub == 6, pltpu.roll(last, 6 - w, 0), tile)
        tile = jnp.where(sub == 7, pltpu.roll(last, 4 - w, 0), tile).astype(BF)
        for k, out in enumerate(outs):
            out[:, span] = tile[m * k : m * k + m]


def add_body(own, one, two, three, out):
    total = (own[...].astype(F32) + one[...].astype(F32)) + (two[...].astype(F32) + three[...].astype(F32))
    out[...] = total.astype(BF)


def sum_body(scale, parts, out):
    total = parts[0:8, :].astype(F32)
    for z in range(1, parts.shape[0] // 8):
        total = total + parts[8 * z : 8 * z + 8, :].astype(F32)
    total = total / scale
    for u in range(6):
        v, w = u // 3, u % 3
        out[u, :, :1536] = total[u : u + 1, :]
        out[u, :, 1536:] = total[6 + v : 7 + v, 512 * w : 512 * w + 512]


def token_body(routes, residual, near, far, out):
    ids = routes[...]
    n = ids.shape[1]
    onehot = (iota((16, n), 0) == ids).astype(F32)
    before = as_bf(iota((n, n), 0) < iota((n, n), 1))
    prefix = dot(onehot.astype(BF), before)
    slot = jnp.sum(onehot * prefix, axis=0, keepdims=True).astype(jnp.int32)
    here = (ids & 1) == lax.axis_index("core")
    k = iota((near.shape[0], n), 0)
    same_near = here & ((k >> 3) == 2 * (ids >> 1))
    c_near = k & 7
    k = iota((far.shape[0], n), 0)
    same_far = jnp.logical_not(here) & ((k >> 3) == (ids >> 1))
    c_far = k & 7
    pick_near = as_bf(same_near & (c_near == slot))
    pick_far = as_bf(same_far & (c_far == slot))
    last_near = near[:, 2048:]
    last_far = far[:, 2048:]
    for r in range(8):
        span = slice(256 * r, 256 * r + 256)
        tail_near = as_bf(same_near & (slot == 8) & (c_near == r))
        tail_far = as_bf(same_far & (slot == 8) & (c_far == r))
        got = dot(pick_near, near[:, span], 0, 0) + dot(pick_far, far[:, span], 0, 0)
        got = got + dot(tail_near, last_near, 0, 0) + dot(tail_far, last_far, 0, 0)
        out[:, span] = (residual[:, span].astype(F32) + got).astype(BF)


def shards(routes, residual_grad, saved_inputs, saved_preact, expert_grad, w_in, w_out):
    S = jax.ShapeDtypeStruct
    slots, width = saved_inputs.shape[1:]
    units = w_in.shape[1]
    groups = lax.axis_size("z") * lax.axis_size("x")
    ids = routes.reshape(1, 128)
    experts = ("y", "core")
    (everyone,) = call(spread_body, [S((16, 128), jnp.int32)], ids, flops=AHEAD)
    everyone = lax.all_to_all(
        everyone.reshape(16, 1, 128), experts, split_axis=0, concat_axis=0, tiled=True
    ).reshape(16, 128)
    (hidden,) = call(
        hidden_body,
        [pltpu.VMEM((slots, units), BF)],
        *[pltpu.with_memory_space_constraint(a[0], pltpu.VMEM) for a in (expert_grad, w_out, saved_preact)],
        flops=2 * slots * units * width,
    )
    slot_grad, spread = call(
        slot_body,
        [S((128, width + 256), BF), pltpu.VMEM((8 * groups, slots), BF)],
        hidden, w_in[0],
        flops=4 * 128 * units * width,
    )
    sends = call(
        weight_body, [S((8 * Z_DEV, 1536), BF)] * X_DEV, spread, saved_inputs[0], everyone,
        flops=2 * slots * 384 * width,
    )
    near = lax.all_to_all(slot_grad, "y", split_axis=0, concat_axis=0, tiled=True)
    far = near.reshape(8, 2, 8, width + 256)[:, 1].reshape(64, width + 256)
    far = lax.ppermute(far, "core", [(0, 1), (1, 0)])
    def shift(i):
        return lax.ppermute(sends[i], "x", [(j, (j + i) % X_DEV) for j in range(X_DEV)])

    (part,) = call(add_body, [S((8 * Z_DEV, 1536), BF)], sends[0], shift(2), shift(1), shift(3))
    part = lax.all_to_all(part, "z", split_axis=0, concat_axis=0, tiled=True)
    (token_grad,) = call(
        token_body, [S((128, width), BF)], ids, residual_grad, near, far,
        flops=6 * 128 * 128 * width,
    )
    token_grad, part = lax.optimization_barrier((token_grad, part))
    (grad_in,) = call(
        functools.partial(sum_body, float(groups)), [S((6, 1, width), F32)], part
    )
    return token_grad, jnp.transpose(grad_in, (1, 0, 2))


def solution(mesh):
    fine = Mesh(mesh.devices.reshape(8, 2, Z_DEV, X_DEV), ("y", "core", "z", "x"))
    tokens = P(("y", "core", "z", "x"), None)
    buffers = P(("y", "core"), ("z", "x"), None)
    weights = P(("y", "core"), None, None)
    return jax.shard_map(
        shards,
        mesh=fine,
        in_specs=(tokens, tokens, buffers, buffers, buffers, weights, weights),
        out_specs=(tokens, buffers),
        check_vma=False,
    )
```

```python
import functools
import math
import jax
import jax.numpy as jnp
from jax import lax
from jax.experimental import pallas as pl
from jax.experimental.pallas import tpu as pltpu
from jax.sharding import Mesh, PartitionSpec as P

BF = jnp.bfloat16
F32 = jnp.float32
CAP = 9
X_DEV = 4
Z_DEV = 12
AHEAD = 10_000_000_000
MIB = 1024 * 1024


def iota(shape, axis):
    return lax.broadcasted_iota(jnp.int32, shape, axis)


def as_bf(mask):
    return mask.astype(F32).astype(BF)


def dot(a, b, ca=1, cb=0):
    return lax.dot_general(a, b, (((ca,), (cb,)), ((), ())), preferred_element_type=F32)


def call(body, outs, *args, flops=0, limit=32, **more):
    size = sum(math.prod(a.shape) * a.dtype.itemsize for a in (*args, *outs))
    return pl.pallas_call(
        body,
        out_shape=outs,
        compiler_params=pltpu.CompilerParams(vmem_limit_bytes=limit * MIB),
        cost_estimate=pl.CostEstimate(flops=flops, bytes_accessed=size, transcendentals=0),
        **more,
    )(*args)


def spread_body(routes, out):
    out[...] = jnp.broadcast_to(routes[...], out.shape)


def hidden_body(grad, w_out, preact, hidden):
    product = dot(grad[...], w_out[...], 1, 1)
    hidden[...] = jnp.where(preact[...].astype(F32) > 0, product, 0.0).astype(BF)


def slot_body(hidden, w_in, slots, spread):
    rows = hidden.shape[0]
    width = w_in.shape[1]
    k = iota((256, rows), 0)
    j = k & 127
    block = 2 * (j >> 4) + (((j >> 3) & 1) ^ lax.axis_index("core"))
    source = CAP * block + jnp.where(k < 128, j & 7, 8)
    picked = dot(as_bf(iota((256, rows), 1) == source), hidden[...]).astype(BF)
    row = iota((128, 256), 0) & 7
    last = jnp.zeros((128, 256), F32)
    for r in range(8):
        span = slice(256 * r, 256 * r + 256)
        got = dot(picked, w_in[:, span])
        slots[:, span] = got[:128].astype(BF)
        last = jnp.where(row == r, got[128:], last)
    slots[:, width:] = last.astype(BF)
    me = lax.axis_index("x")
    units = hidden.shape[1]
    m = spread.shape[0] // X_DEV
    j = iota((m, units), 0)
    unit = iota((m, units), 1)
    for k in range(X_DEV):
        owner = X_DEV * (j >> 3) + ((me + k) & 3)
        place = ((j & 7) < 6) & (unit == 6 * owner + (j & 7))
        spread[m * k : m * k + m, :] = dot(as_bf(place), hidden[...], 1, 1).astype(BF)


def weight_body(spread, inputs, routes, *outs):
    rows = spread.shape[1]
    expert = 2 * lax.axis_index("y") + lax.axis_index("core")
    counts = jnp.sum((routes[...] == expert).astype(F32), axis=1, keepdims=True).astype(jnp.int32)
    n = routes.shape[0]
    g = iota((n, rows), 1)
    first = CAP * iota((n, rows), 0)
    live = (g >= first) & (g < first + counts)
    mask = as_bf(jnp.sum(live.astype(F32), axis=0, keepdims=True) > 0.5)
    gated = spread[...] * mask
    last = dot(gated, inputs[:, 1536:])
    sub = iota(last.shape, 0) & 7
    m = outs[0].shape[0]
    for w in range(3):
        span = slice(512 * w, 512 * w + 512)
        tile = dot(gated, inputs[:, span])
        tile = jnp.where(sub == 6, pltpu.roll(last, 6 - w, 0), tile)
        tile = jnp.where(sub == 7, pltpu.roll(last, 4 - w, 0), tile).astype(BF)
        for k, out in enumerate(outs):
            out[:, span] = tile[m * k : m * k + m]


def add_body(own, two, three, one, out):
    total = (own[...].astype(F32) + one[...].astype(F32)) + (two[...].astype(F32) + three[...].astype(F32))
    out[...] = total.astype(BF)


def sum_body(scale, parts, out):
    total = parts[0:8, :].astype(F32)
    for z in range(1, parts.shape[0] // 8):
        total = total + parts[8 * z : 8 * z + 8, :].astype(F32)
    total = total / scale
    for u in range(6):
        v, w = u // 3, u % 3
        out[u, :, :1536] = total[u : u + 1, :]
        out[u, :, 1536:] = total[6 + v : 7 + v, 512 * w : 512 * w + 512]


def token_body(routes, residual, near, far, out):
    ids = routes[...]
    n = ids.shape[1]
    onehot = (iota((16, n), 0) == ids).astype(F32)
    before = as_bf(iota((n, n), 0) < iota((n, n), 1))
    prefix = dot(onehot.astype(BF), before)
    slot = jnp.sum(onehot * prefix, axis=0, keepdims=True).astype(jnp.int32)
    here = (ids & 1) == lax.axis_index("core")
    k = iota((near.shape[0], n), 0)
    same_near = here & ((k >> 3) == 2 * (ids >> 1))
    c_near = k & 7
    k = iota((far.shape[0], n), 0)
    same_far = jnp.logical_not(here) & ((k >> 3) == (ids >> 1))
    c_far = k & 7
    pick_near = as_bf(same_near & (c_near == slot))
    pick_far = as_bf(same_far & (c_far == slot))
    last_near = near[:, 2048:]
    last_far = far[:, 2048:]
    for r in range(8):
        span = slice(256 * r, 256 * r + 256)
        tail_near = as_bf(same_near & (slot == 8) & (c_near == r))
        tail_far = as_bf(same_far & (slot == 8) & (c_far == r))
        got = dot(pick_near, near[:, span], 0, 0) + dot(pick_far, far[:, span], 0, 0)
        got = got + dot(tail_near, last_near, 0, 0) + dot(tail_far, last_far, 0, 0)
        out[:, span] = (residual[:, span].astype(F32) + got).astype(BF)


def shards(routes, residual_grad, saved_inputs, saved_preact, expert_grad, w_in, w_out):
    S = jax.ShapeDtypeStruct
    slots, width = saved_inputs.shape[1:]
    units = w_in.shape[1]
    groups = lax.axis_size("z") * lax.axis_size("x")
    ids = routes.reshape(1, 128)
    experts = ("y", "core")
    (everyone,) = call(spread_body, [S((16, 128), jnp.int32)], ids, flops=AHEAD)
    everyone = lax.all_to_all(
        everyone.reshape(16, 1, 128), experts, split_axis=0, concat_axis=0, tiled=True
    ).reshape(16, 128)
    (hidden,) = call(
        hidden_body,
        [pltpu.VMEM((slots, units), BF)],
        *[pltpu.with_memory_space_constraint(a[0], pltpu.VMEM) for a in (expert_grad, w_out, saved_preact)],
        flops=2 * slots * units * width,
    )
    slot_grad, spread = call(
        slot_body,
        [S((128, width + 256), BF), pltpu.VMEM((8 * groups, slots), BF)],
        hidden, w_in[0],
        flops=4 * 128 * units * width,
    )
    sends = call(
        weight_body, [S((8 * Z_DEV, 1536), BF)] * X_DEV, spread, saved_inputs[0], everyone,
        flops=2 * slots * 384 * width,
    )
    near = lax.all_to_all(slot_grad, "y", split_axis=0, concat_axis=0, tiled=True)
    far = near.reshape(8, 2, 8, width + 256)[:, 1].reshape(64, width + 256)
    far = lax.ppermute(far, "core", [(0, 1), (1, 0)])
    def shift(i):
        return lax.ppermute(sends[i], "x", [(j, (j + i) % X_DEV) for j in range(X_DEV)])

    (part,) = call(add_body, [S((8 * Z_DEV, 1536), BF)], sends[0], shift(2), shift(3), shift(1))
    part = lax.all_to_all(part, "z", split_axis=0, concat_axis=0, tiled=True)
    (token_grad,) = call(
        token_body, [S((128, width), BF)], ids, residual_grad, near, far,
        flops=6 * 128 * 128 * width,
    )
    token_grad, part = lax.optimization_barrier((token_grad, part))
    (grad_in,) = call(
        functools.partial(sum_body, float(groups)), [S((6, 1, width), F32)], part
    )
    return token_grad, jnp.transpose(grad_in, (1, 0, 2))


def solution(mesh):
    fine = Mesh(mesh.devices.reshape(8, 2, Z_DEV, X_DEV), ("y", "core", "z", "x"))
    tokens = P(("y", "core", "z", "x"), None)
    buffers = P(("y", "core"), ("z", "x"), None)
    weights = P(("y", "core"), None, None)
    return jax.shard_map(
        shards,
        mesh=fine,
        in_specs=(tokens, tokens, buffers, buffers, buffers, weights, weights),
        out_specs=(tokens, buffers),
        check_vma=False,
    )
```

```python
import functools
import math
import jax
import jax.numpy as jnp
from jax import lax
from jax.experimental import pallas as pl
from jax.experimental.pallas import tpu as pltpu
from jax.sharding import Mesh, PartitionSpec as P

BF = jnp.bfloat16
F32 = jnp.float32
CAP = 9
X_DEV = 4
Z_DEV = 12
AHEAD = 10_000_000_000
MIB = 1024 * 1024


def iota(shape, axis):
    return lax.broadcasted_iota(jnp.int32, shape, axis)


def as_bf(mask):
    return mask.astype(F32).astype(BF)


def dot(a, b, ca=1, cb=0):
    return lax.dot_general(a, b, (((ca,), (cb,)), ((), ())), preferred_element_type=F32)


def call(body, outs, *args, flops=0, limit=32, **more):
    size = sum(math.prod(a.shape) * a.dtype.itemsize for a in (*args, *outs))
    return pl.pallas_call(
        body,
        out_shape=outs,
        compiler_params=pltpu.CompilerParams(vmem_limit_bytes=limit * MIB),
        cost_estimate=pl.CostEstimate(flops=flops, bytes_accessed=size, transcendentals=0),
        **more,
    )(*args)


def spread_body(routes, out):
    out[...] = jnp.broadcast_to(routes[...], out.shape)


def hidden_body(grad, w_out, preact, hidden):
    product = dot(grad[...], w_out[...], 1, 1)
    hidden[...] = jnp.where(preact[...].astype(F32) > 0, product, 0.0).astype(BF)


def slot_body(hidden, w_in, slots, spread):
    rows = hidden.shape[0]
    width = w_in.shape[1]
    k = iota((256, rows), 0)
    j = k & 127
    block = 2 * (j >> 4) + (((j >> 3) & 1) ^ lax.axis_index("core"))
    source = CAP * block + jnp.where(k < 128, j & 7, 8)
    picked = dot(as_bf(iota((256, rows), 1) == source), hidden[...]).astype(BF)
    row = iota((128, 256), 0) & 7
    last = jnp.zeros((128, 256), F32)
    for r in range(8):
        span = slice(256 * r, 256 * r + 256)
        got = dot(picked, w_in[:, span])
        slots[:, span] = got[:128].astype(BF)
        last = jnp.where(row == r, got[128:], last)
    slots[:, width:] = last.astype(BF)
    me = lax.axis_index("x")
    units = hidden.shape[1]
    m = spread.shape[0] // X_DEV
    j = iota((m, units), 0)
    unit = iota((m, units), 1)
    for k in range(X_DEV):
        owner = X_DEV * (j >> 3) + (me ^ k)
        place = ((j & 7) < 6) & (unit == 6 * owner + (j & 7))
        spread[m * k : m * k + m, :] = dot(as_bf(place), hidden[...], 1, 1).astype(BF)


def weight_body(spread, inputs, routes, *outs):
    rows = spread.shape[1]
    expert = 2 * lax.axis_index("y") + lax.axis_index("core")
    counts = jnp.sum((routes[...] == expert).astype(F32), axis=1, keepdims=True).astype(jnp.int32)
    n = routes.shape[0]
    g = iota((n, rows), 1)
    first = CAP * iota((n, rows), 0)
    live = (g >= first) & (g < first + counts)
    mask = as_bf(jnp.sum(live.astype(F32), axis=0, keepdims=True) > 0.5)
    gated = spread[...] * mask
    last = dot(gated, inputs[:, 1536:])
    sub = iota(last.shape, 0) & 7
    m = outs[0].shape[0]
    for w in range(3):
        span = slice(512 * w, 512 * w + 512)
        tile = dot(gated, inputs[:, span])
        tile = jnp.where(sub == 6, pltpu.roll(last, 6 - w, 0), tile)
        tile = jnp.where(sub == 7, pltpu.roll(last, 4 - w, 0), tile).astype(BF)
        for k, out in enumerate(outs):
            out[:, span] = tile[m * k : m * k + m]


def add_body(own, two, one, three, out):
    total = (own[...].astype(F32) + two[...].astype(F32)) + (one[...].astype(F32) + three[...].astype(F32))
    out[...] = total.astype(BF)


def sum_body(scale, parts, out):
    total = parts[0:8, :].astype(F32)
    for z in range(1, parts.shape[0] // 8):
        total = total + parts[8 * z : 8 * z + 8, :].astype(F32)
    total = total / scale
    for u in range(6):
        v, w = u // 3, u % 3
        out[u, :, :1536] = total[u : u + 1, :]
        out[u, :, 1536:] = total[6 + v : 7 + v, 512 * w : 512 * w + 512]


def token_body(routes, residual, near, far, out):
    ids = routes[...]
    n = ids.shape[1]
    onehot = (iota((16, n), 0) == ids).astype(F32)
    before = as_bf(iota((n, n), 0) < iota((n, n), 1))
    prefix = dot(onehot.astype(BF), before)
    slot = jnp.sum(onehot * prefix, axis=0, keepdims=True).astype(jnp.int32)
    here = (ids & 1) == lax.axis_index("core")
    k = iota((near.shape[0], n), 0)
    same_near = here & ((k >> 3) == 2 * (ids >> 1))
    c_near = k & 7
    k = iota((far.shape[0], n), 0)
    same_far = jnp.logical_not(here) & ((k >> 3) == (ids >> 1))
    c_far = k & 7
    pick_near = as_bf(same_near & (c_near == slot))
    pick_far = as_bf(same_far & (c_far == slot))
    last_near = near[:, 2048:]
    last_far = far[:, 2048:]
    for r in range(8):
        span = slice(256 * r, 256 * r + 256)
        tail_near = as_bf(same_near & (slot == 8) & (c_near == r))
        tail_far = as_bf(same_far & (slot == 8) & (c_far == r))
        got = dot(pick_near, near[:, span], 0, 0) + dot(pick_far, far[:, span], 0, 0)
        got = got + dot(tail_near, last_near, 0, 0) + dot(tail_far, last_far, 0, 0)
        out[:, span] = (residual[:, span].astype(F32) + got).astype(BF)


def shards(routes, residual_grad, saved_inputs, saved_preact, expert_grad, w_in, w_out):
    S = jax.ShapeDtypeStruct
    slots, width = saved_inputs.shape[1:]
    units = w_in.shape[1]
    groups = lax.axis_size("z") * lax.axis_size("x")
    ids = routes.reshape(1, 128)
    experts = ("y", "core")
    (everyone,) = call(spread_body, [S((16, 128), jnp.int32)], ids, flops=AHEAD)
    everyone = lax.all_to_all(
        everyone.reshape(16, 1, 128), experts, split_axis=0, concat_axis=0, tiled=True
    ).reshape(16, 128)
    (hidden,) = call(
        hidden_body,
        [pltpu.VMEM((slots, units), BF)],
        *[pltpu.with_memory_space_constraint(a[0], pltpu.VMEM) for a in (expert_grad, w_out, saved_preact)],
        flops=2 * slots * units * width,
    )
    slot_grad, spread = call(
        slot_body,
        [S((128, width + 256), BF), pltpu.VMEM((8 * groups, slots), BF)],
        hidden, w_in[0],
        flops=4 * 128 * units * width,
    )
    sends = call(
        weight_body, [S((8 * Z_DEV, 1536), BF)] * X_DEV, spread, saved_inputs[0], everyone,
        flops=2 * slots * 384 * width,
    )
    near = lax.all_to_all(slot_grad, "y", split_axis=0, concat_axis=0, tiled=True)
    far = near.reshape(8, 2, 8, width + 256)[:, 1].reshape(64, width + 256)
    far = lax.ppermute(far, "core", [(0, 1), (1, 0)])
    def swap(k):
        return lax.ppermute(sends[k], "x", [(j, j ^ k) for j in range(X_DEV)])

    (part,) = call(add_body, [S((8 * Z_DEV, 1536), BF)], sends[0], swap(2), swap(1), swap(3))
    part = lax.all_to_all(part, "z", split_axis=0, concat_axis=0, tiled=True)
    (token_grad,) = call(
        token_body, [S((128, width), BF)], ids, residual_grad, near, far,
        flops=6 * 128 * 128 * width,
    )
    token_grad, part = lax.optimization_barrier((token_grad, part))
    (grad_in,) = call(
        functools.partial(sum_body, float(groups)), [S((6, 1, width), F32)], part
    )
    return token_grad, jnp.transpose(grad_in, (1, 0, 2))


def solution(mesh):
    fine = Mesh(mesh.devices.reshape(8, 2, Z_DEV, X_DEV), ("y", "core", "z", "x"))
    tokens = P(("y", "core", "z", "x"), None)
    buffers = P(("y", "core"), ("z", "x"), None)
    weights = P(("y", "core"), None, None)
    return jax.shard_map(
        shards,
        mesh=fine,
        in_specs=(tokens, tokens, buffers, buffers, buffers, weights, weights),
        out_specs=(tokens, buffers),
        check_vma=False,
    )
```

```python
import functools
import math
import jax
import jax.numpy as jnp
from jax import lax
from jax.experimental import pallas as pl
from jax.experimental.pallas import tpu as pltpu
from jax.sharding import Mesh, PartitionSpec as P

BF = jnp.bfloat16
F32 = jnp.float32
CAP = 9
X_DEV = 4
Z_DEV = 12
AHEAD = 10_000_000_000
MIB = 1024 * 1024


def iota(shape, axis):
    return lax.broadcasted_iota(jnp.int32, shape, axis)


def as_bf(mask):
    return mask.astype(F32).astype(BF)


def dot(a, b, ca=1, cb=0):
    return lax.dot_general(a, b, (((ca,), (cb,)), ((), ())), preferred_element_type=F32)


def call(body, outs, *args, flops=0, limit=32, **more):
    size = sum(math.prod(a.shape) * a.dtype.itemsize for a in (*args, *outs))
    return pl.pallas_call(
        body,
        out_shape=outs,
        compiler_params=pltpu.CompilerParams(vmem_limit_bytes=limit * MIB),
        cost_estimate=pl.CostEstimate(flops=flops, bytes_accessed=size, transcendentals=0),
        **more,
    )(*args)


def spread_body(routes, out):
    out[...] = jnp.broadcast_to(routes[...], out.shape)


def hidden_body(grad, w_out, preact, hidden):
    product = dot(grad[...], w_out[...], 1, 1)
    hidden[...] = jnp.where(preact[...].astype(F32) > 0, product, 0.0).astype(BF)


def slot_body(hidden, w_in, slots, spread):
    rows = hidden.shape[0]
    width = w_in.shape[1]
    k = iota((256, rows), 0)
    j = k & 127
    block = 2 * (j >> 4) + (((j >> 3) & 1) ^ lax.axis_index("core"))
    source = CAP * block + jnp.where(k < 128, j & 7, 8)
    picked = dot(as_bf(iota((256, rows), 1) == source), hidden[...]).astype(BF)
    row = iota((128, 256), 0) & 7
    last = jnp.zeros((128, 256), F32)
    for r in range(8):
        span = slice(256 * r, 256 * r + 256)
        got = dot(picked, w_in[:, span])
        slots[:, span] = got[:128].astype(BF)
        last = jnp.where(row == r, got[128:], last)
    slots[:, width:] = last.astype(BF)
    me = lax.axis_index("x")
    units = hidden.shape[1]
    m = spread.shape[0] // X_DEV
    j = iota((m, units), 0)
    unit = iota((m, units), 1)
    for k in range(X_DEV):
        owner = X_DEV * (j >> 3) + (me ^ k)
        place = ((j & 7) < 6) & (unit == 6 * owner + (j & 7))
        spread[m * k : m * k + m, :] = dot(as_bf(place), hidden[...], 1, 1).astype(BF)


def weight_body(spread, inputs, routes, *outs):
    rows = spread.shape[1]
    expert = 2 * lax.axis_index("y") + lax.axis_index("core")
    counts = jnp.sum((routes[...] == expert).astype(F32), axis=1, keepdims=True).astype(jnp.int32)
    n = routes.shape[0]
    g = iota((n, rows), 1)
    first = CAP * iota((n, rows), 0)
    live = (g >= first) & (g < first + counts)
    mask = as_bf(jnp.sum(live.astype(F32), axis=0, keepdims=True) > 0.5)
    gated = spread[...] * mask
    last = dot(gated, inputs[:, 1536:])
    sub = iota(last.shape, 0) & 7
    m = outs[0].shape[0]
    for w in range(3):
        span = slice(512 * w, 512 * w + 512)
        tile = dot(gated, inputs[:, span])
        tile = jnp.where(sub == 6, pltpu.roll(last, 6 - w, 0), tile)
        tile = jnp.where(sub == 7, pltpu.roll(last, 4 - w, 0), tile).astype(BF)
        for k, out in enumerate(outs):
            out[:, span] = tile[m * k : m * k + m]


def add_body(own, two, one, three, out):
    total = (own[...].astype(F32) + two[...].astype(F32)) + (one[...].astype(F32) + three[...].astype(F32))
    out[...] = total.astype(BF)


def sum_body(scale, parts, out):
    every = parts[...].astype(F32)
    total = every[0:8]
    for z in range(1, every.shape[0] // 8):
        total = total + every[8 * z : 8 * z + 8]
    total = total / scale
    for u in range(6):
        v, w = u // 3, u % 3
        out[u, :, :1536] = total[u : u + 1, :]
        out[u, :, 1536:] = total[6 + v : 7 + v, 512 * w : 512 * w + 512]


def token_body(routes, residual, near, far, out):
    ids = routes[...]
    n = ids.shape[1]
    onehot = (iota((16, n), 0) == ids).astype(F32)
    before = as_bf(iota((n, n), 0) < iota((n, n), 1))
    prefix = dot(onehot.astype(BF), before)
    slot = jnp.sum(onehot * prefix, axis=0, keepdims=True).astype(jnp.int32)
    here = (ids & 1) == lax.axis_index("core")
    k = iota((near.shape[0], n), 0)
    same_near = here & ((k >> 3) == 2 * (ids >> 1))
    c_near = k & 7
    k = iota((far.shape[0], n), 0)
    same_far = jnp.logical_not(here) & ((k >> 3) == (ids >> 1))
    c_far = k & 7
    pick_near = as_bf(same_near & (c_near == slot))
    pick_far = as_bf(same_far & (c_far == slot))
    last_near = near[:, 2048:]
    last_far = far[:, 2048:]
    for r in range(8):
        span = slice(256 * r, 256 * r + 256)
        tail_near = as_bf(same_near & (slot == 8) & (c_near == r))
        tail_far = as_bf(same_far & (slot == 8) & (c_far == r))
        got = dot(pick_near, near[:, span], 0, 0) + dot(pick_far, far[:, span], 0, 0)
        got = got + dot(tail_near, last_near, 0, 0) + dot(tail_far, last_far, 0, 0)
        out[:, span] = (residual[:, span].astype(F32) + got).astype(BF)


def shards(routes, residual_grad, saved_inputs, saved_preact, expert_grad, w_in, w_out):
    S = jax.ShapeDtypeStruct
    slots, width = saved_inputs.shape[1:]
    units = w_in.shape[1]
    groups = lax.axis_size("z") * lax.axis_size("x")
    ids = routes.reshape(1, 128)
    experts = ("y", "core")
    (everyone,) = call(spread_body, [S((16, 128), jnp.int32)], ids, flops=AHEAD)
    everyone = lax.all_to_all(
        everyone.reshape(16, 1, 128), experts, split_axis=0, concat_axis=0, tiled=True
    ).reshape(16, 128)
    (hidden,) = call(
        hidden_body,
        [pltpu.VMEM((slots, units), BF)],
        *[pltpu.with_memory_space_constraint(a[0], pltpu.VMEM) for a in (expert_grad, w_out, saved_preact)],
        flops=2 * slots * units * width,
    )
    slot_grad, spread = call(
        slot_body,
        [S((128, width + 256), BF), pltpu.VMEM((8 * groups, slots), BF)],
        hidden, w_in[0],
        flops=4 * 128 * units * width,
    )
    sends = call(
        weight_body, [S((8 * Z_DEV, 1536), BF)] * X_DEV, spread, saved_inputs[0], everyone,
        flops=2 * slots * 384 * width,
    )
    near = lax.all_to_all(slot_grad, "y", split_axis=0, concat_axis=0, tiled=True)
    far = near.reshape(8, 2, 8, width + 256)[:, 1].reshape(64, width + 256)
    far = lax.ppermute(far, "core", [(0, 1), (1, 0)])
    def swap(k):
        return lax.ppermute(sends[k], "x", [(j, j ^ k) for j in range(X_DEV)])

    (part,) = call(add_body, [S((8 * Z_DEV, 1536), BF)], sends[0], swap(2), swap(1), swap(3))
    part = lax.all_to_all(part, "z", split_axis=0, concat_axis=0, tiled=True)
    (token_grad,) = call(
        token_body, [S((128, width), BF)], ids, residual_grad, near, far,
        flops=6 * 128 * 128 * width,
    )
    token_grad, part = lax.optimization_barrier((token_grad, part))
    (grad_in,) = call(
        functools.partial(sum_body, float(groups)), [S((6, 1, width), F32)], part
    )
    return token_grad, jnp.transpose(grad_in, (1, 0, 2))


def solution(mesh):
    fine = Mesh(mesh.devices.reshape(8, 2, Z_DEV, X_DEV), ("y", "core", "z", "x"))
    tokens = P(("y", "core", "z", "x"), None)
    buffers = P(("y", "core"), ("z", "x"), None)
    weights = P(("y", "core"), None, None)
    return jax.shard_map(
        shards,
        mesh=fine,
        in_specs=(tokens, tokens, buffers, buffers, buffers, weights, weights),
        out_specs=(tokens, buffers),
        check_vma=False,
    )
```

```python
import functools
import math
import jax
import jax.numpy as jnp
from jax import lax
from jax.experimental import pallas as pl
from jax.experimental.pallas import tpu as pltpu
from jax.sharding import Mesh, PartitionSpec as P

BF = jnp.bfloat16
F32 = jnp.float32
CAP = 9
X_DEV = 4
Z_DEV = 12
AHEAD = 10_000_000_000
MIB = 1024 * 1024


def iota(shape, axis):
    return lax.broadcasted_iota(jnp.int32, shape, axis)


def as_bf(mask):
    return mask.astype(F32).astype(BF)


def dot(a, b, ca=1, cb=0):
    return lax.dot_general(a, b, (((ca,), (cb,)), ((), ())), preferred_element_type=F32)


def call(body, outs, *args, flops=0, limit=32, **more):
    size = sum(math.prod(a.shape) * a.dtype.itemsize for a in (*args, *outs))
    return pl.pallas_call(
        body,
        out_shape=outs,
        compiler_params=pltpu.CompilerParams(vmem_limit_bytes=limit * MIB),
        cost_estimate=pl.CostEstimate(flops=flops, bytes_accessed=size, transcendentals=0),
        **more,
    )(*args)


def spread_body(routes, out):
    out[...] = jnp.broadcast_to(routes[...], out.shape)


def hidden_body(grad, w_out, preact, hidden):
    product = dot(grad[...], w_out[...], 1, 1)
    hidden[...] = jnp.where(preact[...].astype(F32) > 0, product, 0.0).astype(BF)


def slot_body(hidden, w_in, slots, spread):
    rows = hidden.shape[0]
    width = w_in.shape[1]
    k = iota((256, rows), 0)
    j = k & 127
    block = 2 * (j >> 4) + (((j >> 3) & 1) ^ lax.axis_index("core"))
    source = CAP * block + jnp.where(k < 128, j & 7, 8)
    picked = dot(as_bf(iota((256, rows), 1) == source), hidden[...]).astype(BF)
    row = iota((128, 256), 0) & 7
    last = jnp.zeros((128, 256), F32)
    for r in range(8):
        span = slice(256 * r, 256 * r + 256)
        got = dot(picked, w_in[:, span])
        slots[:, span] = got[:128].astype(BF)
        last = jnp.where(row == r, got[128:], last)
    slots[:, width:] = last.astype(BF)
    me = lax.axis_index("x")
    units = hidden.shape[1]
    m = spread.shape[0] // X_DEV
    j = iota((m, units), 0)
    unit = iota((m, units), 1)
    for k in range(X_DEV):
        owner = X_DEV * (j >> 3) + (me ^ k)
        place = ((j & 7) < 6) & (unit == 6 * owner + (j & 7))
        spread[m * k : m * k + m, :] = dot(as_bf(place), hidden[...], 1, 1).astype(BF)


def weight_body(spread, inputs, routes, *outs):
    rows = spread.shape[1]
    expert = 2 * lax.axis_index("y") + lax.axis_index("core")
    counts = jnp.sum((routes[...] == expert).astype(F32), axis=1, keepdims=True).astype(jnp.int32)
    n = routes.shape[0]
    g = iota((n, rows), 1)
    first = CAP * iota((n, rows), 0)
    live = (g >= first) & (g < first + counts)
    mask = as_bf(jnp.sum(live.astype(F32), axis=0, keepdims=True) > 0.5)
    gated = spread[...] * mask
    last = dot(gated, inputs[:, 1536:])
    sub = iota(last.shape, 0) & 7
    m = outs[0].shape[0]
    for w in range(3):
        span = slice(512 * w, 512 * w + 512)
        tile = dot(gated, inputs[:, span])
        tile = jnp.where(sub == 6, pltpu.roll(last, 6 - w, 0), tile)
        tile = jnp.where(sub == 7, pltpu.roll(last, 4 - w, 0), tile).astype(BF)
        for k, out in enumerate(outs):
            out[:, span] = tile[m * k : m * k + m]


def sum_body(scale, parts, out):
    every = parts[...].astype(F32)
    total = every[0:8]
    for z in range(1, every.shape[0] // 8):
        total = total + every[8 * z : 8 * z + 8]
    total = total / scale
    for u in range(6):
        v, w = u // 3, u % 3
        out[u, :, :1536] = total[u : u + 1, :]
        out[u, :, 1536:] = total[6 + v : 7 + v, 512 * w : 512 * w + 512]


def token_body(routes, residual, near, far, out):
    ids = routes[...]
    n = ids.shape[1]
    onehot = (iota((16, n), 0) == ids).astype(F32)
    before = as_bf(iota((n, n), 0) < iota((n, n), 1))
    prefix = dot(onehot.astype(BF), before)
    slot = jnp.sum(onehot * prefix, axis=0, keepdims=True).astype(jnp.int32)
    here = (ids & 1) == lax.axis_index("core")
    k = iota((near.shape[0], n), 0)
    same_near = here & ((k >> 3) == 2 * (ids >> 1))
    c_near = k & 7
    k = iota((far.shape[0], n), 0)
    same_far = jnp.logical_not(here) & ((k >> 3) == (ids >> 1))
    c_far = k & 7
    pick_near = as_bf(same_near & (c_near == slot))
    pick_far = as_bf(same_far & (c_far == slot))
    last_near = near[:, 2048:]
    last_far = far[:, 2048:]
    for r in range(8):
        span = slice(256 * r, 256 * r + 256)
        tail_near = as_bf(same_near & (slot == 8) & (c_near == r))
        tail_far = as_bf(same_far & (slot == 8) & (c_far == r))
        got = dot(pick_near, near[:, span], 0, 0) + dot(pick_far, far[:, span], 0, 0)
        got = got + dot(tail_near, last_near, 0, 0) + dot(tail_far, last_far, 0, 0)
        out[:, span] = (residual[:, span].astype(F32) + got).astype(BF)


def shards(routes, residual_grad, saved_inputs, saved_preact, expert_grad, w_in, w_out):
    S = jax.ShapeDtypeStruct
    slots, width = saved_inputs.shape[1:]
    units = w_in.shape[1]
    groups = lax.axis_size("z") * lax.axis_size("x")
    ids = routes.reshape(1, 128)
    experts = ("y", "core")
    (everyone,) = call(spread_body, [S((16, 128), jnp.int32)], ids, flops=AHEAD)
    everyone = lax.all_to_all(
        everyone.reshape(16, 1, 128), experts, split_axis=0, concat_axis=0, tiled=True
    ).reshape(16, 128)
    (hidden,) = call(
        hidden_body,
        [pltpu.VMEM((slots, units), BF)],
        *[pltpu.with_memory_space_constraint(a[0], pltpu.VMEM) for a in (expert_grad, w_out, saved_preact)],
        flops=2 * slots * units * width,
    )
    slot_grad, spread = call(
        slot_body,
        [S((128, width + 256), BF), pltpu.VMEM((8 * groups, slots), BF)],
        hidden, w_in[0],
        flops=4 * 128 * units * width,
    )
    sends = call(
        weight_body, [S((8 * Z_DEV, 1536), BF)] * X_DEV, spread, saved_inputs[0], everyone,
        flops=2 * slots * 384 * width,
    )
    near = lax.all_to_all(slot_grad, "y", split_axis=0, concat_axis=0, tiled=True)
    far = near.reshape(8, 2, 8, width + 256)[:, 1].reshape(64, width + 256)
    far = lax.ppermute(far, "core", [(0, 1), (1, 0)])
    def swap(k):
        return lax.ppermute(sends[k], "x", [(j, j ^ k) for j in range(X_DEV)])

    two, one, three = [swap(k).astype(F32) for k in (2, 1, 3)]
    part = ((sends[0].astype(F32) + two) + (one + three)).astype(BF)
    part = lax.all_to_all(part, "z", split_axis=0, concat_axis=0, tiled=True)
    (token_grad,) = call(
        token_body, [S((128, width), BF)], ids, residual_grad, near, far,
        flops=6 * 128 * 128 * width,
    )
    token_grad, part = lax.optimization_barrier((token_grad, part))
    (grad_in,) = call(
        functools.partial(sum_body, float(groups)), [S((6, 1, width), F32)], part
    )
    return token_grad, jnp.transpose(grad_in, (1, 0, 2))


def solution(mesh):
    fine = Mesh(mesh.devices.reshape(8, 2, Z_DEV, X_DEV), ("y", "core", "z", "x"))
    tokens = P(("y", "core", "z", "x"), None)
    buffers = P(("y", "core"), ("z", "x"), None)
    weights = P(("y", "core"), None, None)
    return jax.shard_map(
        shards,
        mesh=fine,
        in_specs=(tokens, tokens, buffers, buffers, buffers, weights, weights),
        out_specs=(tokens, buffers),
        check_vma=False,
    )
```
